32 devices in a mesh: seq: 8 (over z, y), mp: 4 (over x, core).
Axes of the slice: x: 2, y: 2, z: 4, core: 2. Of those that a mesh axis runs over, the one named last changes fastest.
Arguments:
- latents: bfloat16 [16, 128, 256], P('seq'), may hold values from -6 to 6
- conv_w: bfloat16 [3, 3, 256, 256], P(None, None, None, 'mp'), may hold values from -0.125 to 0.125
- embed_w: bfloat16 [4, 256, 4096], P(None, 'mp', 'seq'), may hold values from -0.1875 to 0.1875
- text_emb: bfloat16 [1024, 4096], P('seq', 'mp'), may hold values from -6 to 6
- wqkv: bfloat16 [4096, 3, 2048], P(None, None, 'mp'), may hold values from -2 to 2
- seg_ids: int32 [1024], replicated, may hold values from 0 to 1, as said below
Outputs:
- attn: bfloat16 [1024, 2048], P('seq', 'mp')
The draws below stay inside these ranges and needn't reach their ends.
Inputs may be any that keep to these rules, and one draw needn't show every extreme that they name: `seg_ids`: image n occupies one run of 512 positions that starts at a multiple of 64; runs come in the order of n and every image is present; 0 marks text.
All inputs are finite; a program needn't handle non-finite values.
Results may differ from the reference program's by a relative error of at most 0.015.
The reference program's roundings to bfloat16 on the way count: a program that leaves them out, or rounds other values in their place, can miss the bound.
Values may be sent and summed in bfloat16 or wider, within the bound.
A program may use at most 128 MiB of HBM per device.

```python
import math
import jax
import jax.numpy as jnp
from jax import lax

D = 4096
HEADS = 16
HD = 128
C = 256
PCOLS = 64
IMG_ROWS = 8
SEQLEN = 1024
NIMG = 1


def draw_seg_ids(key, part):
    key = jax.random.fold_in(key, 11)
    units = SEQLEN // PCOLS
    spare = units - NIMG * IMG_ROWS
    offsets = jnp.sort(jax.random.randint(key, (NIMG,), 0, spare + 1))
    starts = offsets * PCOLS + jnp.arange(NIMG, dtype=jnp.int32) * (IMG_ROWS * PCOLS)
    positions = jnp.arange(SEQLEN, dtype=jnp.int32)
    inside = (positions[None, :] >= starts[:, None]) & (positions[None, :] < starts[:, None] + IMG_ROWS * PCOLS)
    labels = jnp.arange(1, NIMG + 1, dtype=jnp.int32)
    return jnp.sum(jnp.where(inside, labels[:, None], 0), axis=0).astype(jnp.int32)


def shared_basis(key):
    basis_key = jax.random.fold_in(key, 29)
    first_key, second_key, third_key = jax.random.split(basis_key, 3)
    query_sign = (2 * jax.random.randint(first_key, (D,), 0, 2) - 1).astype(jnp.float32)
    key_sign = (2 * jax.random.randint(second_key, (D,), 0, 2) - 1).astype(jnp.float32)
    head_dirs = jnp.clip(jax.random.normal(third_key, (HEADS, HD), jnp.float32), -3.0, 3.0)
    return (query_sign, key_sign, head_dirs)


def chosen_rows(key, part):
    segments = draw_seg_ids(key, part)
    row_key = jax.random.fold_in(key, 31)
    positions = jnp.arange(SEQLEN, dtype=jnp.int32)
    ranks = jax.random.randint(row_key, (SEQLEN,), 0, 1024)
    marks = jnp.where(segments == 0, ranks * SEQLEN + positions, -1)
    picked = lax_top(marks)
    return picked


def lax_top(marks):
    return jax.lax.top_k(marks, 20)[1].astype(jnp.int32)


def draw_text_emb(key, part):
    query_sign, key_sign, head_dirs = shared_basis(key)
    picked = chosen_rows(key, part)
    key = jax.random.fold_in(key, 17)
    drawn_key, strength_key, query_key = jax.random.split(key, 3)
    drawn = jnp.clip(jax.random.normal(drawn_key, (SEQLEN, D), jnp.float32), -6.0, 6.0)
    key_strength = jax.random.uniform(strength_key, (16,), jnp.float32, 0.9, 1.1)
    query_strength = jax.random.uniform(query_key, (4,), jnp.float32, 2.5, 3.5)
    positions = jnp.arange(SEQLEN, dtype=jnp.int32)
    key_hit = positions[:, None] == picked[None, :16]
    query_hit = positions[:, None] == picked[None, 16:]
    key_scale = jnp.sum(jnp.where(key_hit, key_strength[None, :], 0.0), axis=1)
    query_scale = jnp.sum(jnp.where(query_hit, query_strength[None, :], 0.0), axis=1)
    is_key = jnp.any(key_hit, axis=1)
    is_query = jnp.any(query_hit, axis=1)
    rows = jnp.where(is_key[:, None], key_scale[:, None] * key_sign[None, :] + 0.3 * drawn, drawn)
    rows = jnp.where(is_query[:, None], query_scale[:, None] * query_sign[None, :], rows)
    return rows.astype(jnp.bfloat16)


def draw_wqkv(key, part):
    query_sign, key_sign, head_dirs = shared_basis(key)
    key = jax.random.fold_in(key, 23)
    base = jnp.clip(jax.random.normal(key, (D, 3, HEADS * HD), jnp.float32), -6.0, 6.0) * D ** (-0.5)
    part_gain = jnp.array([1.7, 1.7, 1.0], jnp.float32)
    base = base * part_gain[None, :, None]
    query_gain = 0.115 * math.sqrt(D)
    key_gain = 1.0
    flat_dirs = head_dirs.reshape(HEADS * HD)
    query_part = query_gain / D * query_sign[:, None] * flat_dirs[None, :]
    key_part = key_gain / D * key_sign[:, None] * flat_dirs[None, :]
    planted = jnp.stack([query_part, key_part, jnp.zeros_like(query_part)], axis=1)
    return (base + planted).astype(jnp.bfloat16)


def block_levels(key, dims, cuts, low, high):
    gain = 1.0
    for axis_at, parts in cuts:
        steps = jax.random.uniform(jax.random.fold_in(jax.random.fold_in(key, 6), axis_at), (parts,), jnp.float32, low / len(cuts), high / len(cuts))
        gain = gain * jnp.repeat(jnp.exp(steps), dims[axis_at] // parts).reshape((-1,) + (1,) * (len(dims) - 1 - axis_at))
    return gain


def centred(stream_key, dims, deviation, limit, cuts=(), kind=jnp.bfloat16):
    factor_of = block_levels(stream_key, dims, cuts, -0.22, 0.18) if cuts else 1.0
    values = jax.random.normal(stream_key, dims, jnp.float32) * deviation * factor_of
    return jnp.minimum(jnp.maximum(values, -limit), limit).astype(kind)


def setup_inputs(seed: int = 0) -> dict:
    streams_of = jax.random.split(jax.random.key(seed), 7)
    return {
        "latents": centred(streams_of[0], (NIMG * 2 * IMG_ROWS, 2 * PCOLS, C), 1.0, 6.0, ((0, 8),)),
        "conv_w": centred(streams_of[1], (3, 3, C, C), (9 * C) ** -0.5, 0.125, ((3, 4),)),
        "embed_w": centred(streams_of[2], (4, C, D), (4 * C) ** -0.5, 0.1875, ((1, 4), (2, 8))),
        "text_emb": draw_text_emb(jax.random.fold_in(streams_of[6], 71), 0),
        "wqkv": draw_wqkv(jax.random.fold_in(streams_of[6], 71), 0),
        "seg_ids": draw_seg_ids(jax.random.fold_in(streams_of[6], 71), 0),
    }


def image_starts(seg_ids):
    positions = jnp.arange(SEQLEN, dtype=jnp.int32)
    labels = jnp.arange(1, NIMG + 1, dtype=jnp.int32)
    marks = seg_ids[None, :] == labels[:, None]
    return jnp.min(jnp.where(marks, positions[None, :], SEQLEN), axis=1).astype(jnp.int32)


def down_block(latents, conv_w):
    images = latents.reshape(NIMG, 2 * IMG_ROWS, 2 * PCOLS, C)
    padded = jnp.pad(images, ((0, 0), (1, 1), (1, 1), (0, 0)))
    summed = jnp.zeros((NIMG, 2 * IMG_ROWS, 2 * PCOLS, C), jnp.float32)
    for row_step in range(3):
        for col_step in range(3):
            window = padded[:, row_step:row_step + 2 * IMG_ROWS, col_step:col_step + 2 * PCOLS, :]
            summed = summed + jnp.einsum("nhwc,cd->nhwd", window.astype(jnp.float32), conv_w[row_step, col_step].astype(jnp.float32))
    return (images.astype(jnp.float32) + jax.nn.silu(summed)).astype(jnp.bfloat16)


def reference(latents, conv_w, embed_w, text_emb, wqkv, seg_ids):
    mixed = down_block(latents, conv_w)
    tiles = mixed.reshape(NIMG, IMG_ROWS, 2, PCOLS, 2, C).transpose(0, 1, 3, 2, 4, 5).reshape(NIMG * IMG_ROWS * PCOLS, 4 * C)
    embedded = jnp.dot(tiles, embed_w.reshape(4 * C, D), preferred_element_type=jnp.float32).astype(jnp.bfloat16)
    starts = image_starts(seg_ids)
    inner = jnp.arange(IMG_ROWS * PCOLS, dtype=jnp.int32)
    targets = (starts[:, None] + inner[None, :]).reshape(-1)
    hidden = text_emb.at[targets].set(embedded)
    qkv = jnp.dot(hidden, wqkv.reshape(D, 3 * HEADS * HD), preferred_element_type=jnp.float32).astype(jnp.bfloat16)
    qkv = qkv.reshape(SEQLEN, 3, HEADS, HD)
    queries = qkv[:, 0].astype(jnp.float32)
    keys = qkv[:, 1].astype(jnp.float32)
    values = qkv[:, 2].astype(jnp.float32)
    block_rows = 512 if SEQLEN % 512 == 0 else SEQLEN
    key_pos = jnp.arange(SEQLEN, dtype=jnp.int32)
    scale = HD ** -0.5

    def attend(block):
        first = (block * block_rows).astype(jnp.int32)
        query_blk = lax.dynamic_slice_in_dim(queries, first, block_rows, 0)
        query_pos = first + jnp.arange(block_rows, dtype=jnp.int32)
        query_seg = lax.dynamic_slice_in_dim(seg_ids, first, block_rows, 0)
        allowed = (key_pos[None, :] <= query_pos[:, None]) | ((query_seg[:, None] == seg_ids[None, :]) & (query_seg[:, None] > 0))
        scores = jnp.einsum("qhd,khd->hqk", query_blk, keys) * scale
        scores = jnp.where(allowed[None], scores, -1e30)
        highest = jnp.max(scores, axis=-1)
        weights = jnp.where(allowed[None], jnp.exp(scores - highest[..., None]), 0.0)
        totals = jnp.sum(weights, axis=-1)
        probs = lax.optimization_barrier(weights.astype(jnp.bfloat16)).astype(jnp.float32)
        result = jnp.einsum("hqk,khd->hqd", probs, values) / totals[..., None]
        return result.transpose(1, 0, 2).reshape(block_rows, HEADS * HD).astype(jnp.bfloat16)

    blocks = lax.map(attend, jnp.arange(SEQLEN // block_rows, dtype=jnp.int32))
    return blocks.reshape(SEQLEN, HEADS * HD)
```

```python
import functools

import jax
import jax.numpy as jnp
from jax import lax
from jax.experimental import pallas as pl
from jax.experimental.pallas import tpu as pltpu
from jax.sharding import PartitionSpec as P

HD = 128


def padded_2(cells, sides, width):
    for axis, dim in sides:
        count = lax.axis_size(axis)
        ends = count - 1
        head = lax.slice_in_dim(cells, 0, width, axis=dim)
        tail = lax.slice_in_dim(cells, cells.shape[dim] - width, cells.shape[dim], axis=dim)
        cells = jnp.concatenate(
            [
                lax.ppermute(tail, axis, [(i, (i + 1) % count) for i in range(ends)]),
                cells,
                lax.ppermute(head, axis, [((i + 1) % count, i) for i in range(ends)]),
            ],
            axis=dim,
        )
    return cells


def attend_block(carry, pieces, queries, query_pos, query_seg, seg_ids, scale):
    running, totals, outputs = carry
    key_blk, value_blk = pieces
    count = key_blk.shape[0]
    heads = queries.shape[1]
    head_size = queries.shape[2]
    key_heads = key_blk.reshape(count, heads, head_size)
    value_heads = value_blk.reshape(count, heads, head_size)
    key_pos = jnp.arange(count, dtype=jnp.int32)
    allowed = (key_pos[None, :] <= query_pos[:, None]) | (
        query_seg[:, None] == seg_ids[None, :]
    ) & (query_seg[:, None] > 0)
    scores = (
        jnp.einsum("qhd,khd->hqk", queries, key_heads, preferred_element_type=jnp.float32) * scale
    )
    scores = jnp.where(allowed[None], scores, -1e30)
    updated = jnp.maximum(running, jnp.max(scores, axis=-1))
    weights = jnp.where(allowed[None], jnp.exp(scores - updated[..., None]), 0.0)
    totals = jnp.sum(weights, axis=-1)
    probs = weights.astype(jnp.bfloat16)
    outputs = jnp.einsum("hqk,khd->hqd", probs, value_heads, preferred_element_type=jnp.float32)
    return (updated, totals, outputs)


def shards(latents, conv_w, embed_w, text_emb, wqkv, seg_ids):
    tile_rows = latents.shape[0]
    tile_cols = latents.shape[1]
    channels = latents.shape[2]
    chan_dev = conv_w.shape[3]
    patch_rows = tile_rows // 2
    patch_cols = tile_cols // 2
    seq_count = lax.axis_size("seq")
    image_rows = seq_count * patch_rows
    num_images = 1
    tok_rows = text_emb.shape[0]
    total_len = seg_ids.shape[0]
    seq_index = lax.axis_index("seq")
    mp_index = lax.axis_index("mp")
    extended = padded_2(latents, (("seq", 0),), 1)
    first_row = seq_index * tile_rows
    image_height = 2 * image_rows
    keep_top = first_row % image_height != 0
    keep_bottom = (first_row + tile_rows) % image_height != 0
    row_ids = jnp.arange(tile_rows + 2, dtype=jnp.int32)
    keep = jnp.where(row_ids == 0, keep_top, jnp.where(row_ids == tile_rows + 1, keep_bottom, True))
    extended = jnp.where(keep[:, None, None], extended, jnp.zeros_like(extended))
    padded = jnp.pad(extended, ((0, 0), (1, 1), (0, 0)))
    summed = jnp.zeros((tile_rows * tile_cols, chan_dev), jnp.float32)
    for row_step in range(3):
        for col_step in range(3):
            window = padded[
                row_step : row_step + tile_rows, col_step : col_step + tile_cols, :
            ].reshape(tile_rows * tile_cols, channels)
            summed = summed + jnp.dot(
                window, conv_w[row_step, col_step], preferred_element_type=jnp.float32
            )
    own_chan = lax.dynamic_slice_in_dim(latents, mp_index * chan_dev, chan_dev, 2)
    mixed = (
        own_chan.astype(jnp.float32) + jax.nn.silu(summed.reshape(tile_rows, tile_cols, chan_dev))
    ).astype(jnp.bfloat16)
    patches = (
        mixed.reshape(patch_rows, 2, patch_cols, 2, chan_dev)
        .transpose(0, 2, 1, 3, 4)
        .reshape(patch_rows * patch_cols, 4 * chan_dev)
    )
    positions = jnp.arange(total_len, dtype=jnp.int32)
    labels = jnp.arange(1, num_images + 1, dtype=jnp.int32)
    marks = seg_ids[None, :] == labels[:, None]
    starts = jnp.min(jnp.where(marks, positions[None, :], total_len), axis=1)
    base = seq_index * tok_rows
    my_pos = base + jnp.arange(tok_rows, dtype=jnp.int32)
    piece = lax.all_gather(patches, "seq", axis=0, tiled=True)
    count = piece.shape[0]
    token = jnp.arange(count, dtype=jnp.int32)
    row_glob = token // patch_cols
    column = token % patch_cols
    image = row_glob // image_rows
    inner = row_glob % image_rows
    begin = jnp.sum(jnp.where(image[:, None] == labels[None, :] - 1, starts[None, :], 0), axis=1)
    target = begin + inner * patch_cols + column
    select = (my_pos[:, None] == target[None, :]).astype(jnp.bfloat16)
    placed = jnp.dot(select, piece, preferred_element_type=jnp.float32).astype(jnp.bfloat16)
    piece = lax.all_gather(embed_w, "seq", axis=2, tiled=True)
    partial_emb = jnp.dot(
        placed, piece.reshape(4 * chan_dev, piece.shape[2]), preferred_element_type=jnp.float32
    )
    my_seg = lax.dynamic_slice_in_dim(seg_ids, base, tok_rows, 0)
    is_text = my_seg == 0
    feat_dev = text_emb.shape[1]
    text_part = jnp.where(is_text[:, None], text_emb.astype(jnp.float32), 0.0)
    own_cols = lax.dynamic_slice_in_dim(partial_emb, mp_index * feat_dev, feat_dev, 1)
    partial_emb = lax.dynamic_update_slice_in_dim(
        partial_emb, own_cols + text_part, mp_index * feat_dev, 1
    )
    hidden = lax.psum(partial_emb, "mp").astype(jnp.bfloat16)
    width = wqkv.shape[0]
    head_cols = wqkv.shape[2]
    head_size = HD
    heads_dev = head_cols // head_size
    qkv = jnp.dot(
        hidden, wqkv.reshape(width, 3 * head_cols), preferred_element_type=jnp.float32
    ).astype(jnp.bfloat16)
    qkv = qkv.reshape(tok_rows, 3, head_cols)
    queries = qkv[:, 0].reshape(tok_rows, heads_dev, head_size)
    key_rows = qkv[:, 1]
    value_rows = qkv[:, 2]
    scale = head_size ** (-0.5)
    fold_init = (
        jnp.full((heads_dev, tok_rows), -1e30, jnp.float32),
        jnp.zeros((heads_dev, tok_rows), jnp.float32),
        jnp.zeros((heads_dev, tok_rows, head_size), jnp.float32),
    )
    running, totals, outputs = attend_block(
        fold_init,
        (
            lax.all_gather(key_rows, "seq", axis=0, tiled=True),
            lax.all_gather(value_rows, "seq", axis=0, tiled=True),
        ),
        queries,
        my_pos,
        my_seg,
        seg_ids,
        scale,
    )
    result = outputs / totals[..., None]
    return result.transpose(1, 0, 2).reshape(tok_rows, heads_dev * head_size).astype(jnp.bfloat16)


def fused_kernel(
    n_s,
    n_m,
    groups,
    seg_ref,
    lat_ref,
    conv_ref,
    embed_ref,
    text_ref,
    w_ref,
    out_ref,
    w_buf,
    halo,
    ew,
    text_buf,
    patch_buf,
    emb_pad,
    emb_out,
    hid_buf,
    acc,
    qkv_out,
    qkv_buf,
    attn_out,
    attn_buf,
    w_sem,
    halo_send,
    halo_recv,
    ew_send,
    ew_recv,
    text_send,
    text_recv,
    patch_send,
    patch_recv,
    hid_send,
    hid_recv,
    qkv_send,
    qkv_recv,
    attn_send,
    attn_recv,
):
    ranks = n_s // groups
    s = lax.axis_index("seq")
    m = lax.axis_index("mp")
    g = s // ranks
    r = s % ranks
    far = (m + 2) % n_m
    near = m + 1 - 2 * (m % 2)
    cols = lat_ref.shape[1]
    chans = lat_ref.shape[2]
    chan_dev = conv_ref.shape[2]
    half = cols // 2
    tok_rows = text_ref.shape[0]
    width = ew.shape[2]
    img_toks = n_s * half
    total_len = n_s * tok_rows
    pending = []

    def push(src, dst, send, recv, seq, mp):
        copy = pltpu.make_async_remote_copy(
            src_ref=src,
            dst_ref=dst,
            send_sem=send,
            recv_sem=recv,
            device_id=(seq, mp),
            device_id_type=pl.DeviceIdType.MESH,
        )
        copy.start()
        pending.append(copy)

    def arrived(dst, send, recv):
        pltpu.make_async_remote_copy(
            src_ref=dst,
            dst_ref=dst,
            send_sem=send,
            recv_sem=recv,
            device_id=(s, near),
            device_id_type=pl.DeviceIdType.MESH,
        ).wait_recv()

    w_copies = [
        pltpu.make_async_copy(w_ref.at[part], w_buf.at[part], w_sem.at[part]) for part in range(3)
    ]
    for copy in w_copies:
        copy.start()

    barrier = pltpu.get_barrier_semaphore()
    for step in range(1, n_s):
        pl.semaphore_signal(
            barrier, 1, device_id=((s + step) % n_s, m), device_id_type=pl.DeviceIdType.MESH
        )
    for step in range(1, n_m):
        pl.semaphore_signal(
            barrier, 1, device_id=(s, (m + step) % n_m), device_id_type=pl.DeviceIdType.MESH
        )
    pl.semaphore_wait(barrier, n_s + n_m - 2)

    def edge(first, seq):
        return pltpu.make_async_remote_copy(
            src_ref=lat_ref.at[1 - first],
            dst_ref=halo.at[first],
            send_sem=halo_send.at[first],
            recv_sem=halo_recv.at[first],
            device_id=(seq, m),
            device_id_type=pl.DeviceIdType.MESH,
        )

    @pl.when(s < n_s - 1)
    def _():
        edge(0, s + 1).start()

    @pl.when(s > 0)
    def _():
        edge(1, s - 1).start()

    for step in range(1, n_m):
        peer = (m + step) % n_m
        push(
            embed_ref.at[:, pl.ds(pl.multiple_of(peer * width, width), width)],
            ew.at[m],
            ew_send.at[step - 1],
            ew_recv.at[m],
            s,
            peer,
        )
    ew[m] = embed_ref[:, pl.ds(pl.multiple_of(m * width, width), width)]
    push(text_ref, text_buf.at[m], text_send.at[0], text_recv.at[m], s, far)
    push(text_ref, text_buf.at[m], text_send.at[1], text_recv.at[m], s, near)
    text_buf[m] = text_ref[...]

    start_unit = jnp.int32(0)
    before = jnp.int32(1)
    for unit in range((total_len - img_toks) // half):
        before = before * (1 - seg_ref[unit * half])
        start_unit = start_unit + before
    start = start_unit * half

    zero_row = jnp.zeros((cols, chans), jnp.bfloat16)

    @pl.when(s == 0)
    def _():
        halo[0] = zero_row

    @pl.when(s == n_s - 1)
    def _():
        halo[1] = zero_row

    def one_hot(rows, columns, shift):
        row = lax.broadcasted_iota(jnp.int32, (rows, columns), 0)
        column = lax.broadcasted_iota(jnp.int32, (rows, columns), 1)
        return jnp.where(column == shift(row), 1.0, 0.0).astype(jnp.bfloat16)

    picks = one_hot(4 * half, cols, lambda row: 2 * (row % half) + row // half - 1)

    def picked(row):
        return jnp.dot(picks, row, preferred_element_type=jnp.float32).astype(jnp.bfloat16)

    inner_rows = [picked(lat_ref[0]), picked(lat_ref[1])]

    @pl.when(s > 0)
    def _():
        edge(0, s).wait_recv()

    @pl.when(s < n_s - 1)
    def _():
        edge(1, s).wait_recv()

    rows = [picked(halo[0]), *inner_rows, picked(halo[1])]
    summed = jnp.zeros((4 * half, chan_dev), jnp.float32)
    for row_step in range(3):
        for col_step in range(3):
            at = slice(col_step * half, (col_step + 2) * half)
            window = jnp.concatenate([rows[row_step][at], rows[row_step + 1][at]], axis=0)
            summed = summed + lax.dot_general(
                window,
                conv_ref[row_step, col_step],
                (((1,), (1,)), ((), ())),
                preferred_element_type=jnp.float32,
            )
    at = slice(half, 3 * half)
    centre = jnp.concatenate([rows[1][at], rows[2][at]], axis=0)
    row = lax.broadcasted_iota(jnp.int32, (chans, chan_dev), 0)
    column = lax.broadcasted_iota(jnp.int32, (chans, chan_dev), 1)
    own = jnp.where(row == column + m * chan_dev, 1.0, 0.0).astype(jnp.bfloat16)
    own_chan = jnp.dot(centre, own, preferred_element_type=jnp.float32)
    mixed = (own_chan + summed / (1.0 + jnp.exp(-summed))).astype(jnp.bfloat16)
    patches = jnp.zeros((half, 4 * chan_dev), jnp.float32)
    for cell in range(4):
        place = one_hot(chan_dev, 4 * chan_dev, lambda row: row + cell * chan_dev)
        patches = patches + jnp.dot(
            mixed[cell * half : (cell + 1) * half], place, preferred_element_type=jnp.float32
        )
    patch_buf[s, m] = patches.astype(jnp.bfloat16)

    sent = [0]

    def send_patch(slot_s, slot_m, seq, mp):
        push(
            patch_buf.at[slot_s, slot_m],
            patch_buf.at[slot_s, slot_m],
            patch_send.at[sent[0]],
            patch_recv.at[slot_s, slot_m],
            seq,
            mp,
        )
        sent[0] += 1

    def wait_patch(slot_s, slot_m):
        arrived(patch_buf.at[slot_s, slot_m], patch_send.at[0], patch_recv.at[slot_s, slot_m])

    for step in range(1, groups):
        send_patch(s, m, (g + step) % groups * ranks + r, m)
    for group_step in range(groups):
        slot = (g + group_step) % groups * ranks + r
        if group_step:
            wait_patch(slot, m)
        for step in range(1, ranks):
            send_patch(slot, m, g * ranks + (r + step) % ranks, m)
        send_patch(slot, m, s, far)
        send_patch(slot, m, s, near)
    for group_step in range(groups):
        for step in range(1, ranks):
            slot = (g + group_step) % groups * ranks + (r + step) % ranks
            wait_patch(slot, m)
            send_patch(slot, m, s, far)
            send_patch(slot, m, s, near)
    for step in range(n_s):
        slot = (s + step) % n_s
        wait_patch(slot, far)
        send_patch(slot, far, s, near)

    arrived(text_buf.at[far], text_send.at[0], text_recv.at[far])
    push(text_buf.at[far], text_buf.at[far], text_send.at[2], text_recv.at[far], s, near)
    near_far = (near + 2) % n_m

    for step in range(1, n_m):
        peer = (m + step) % n_m
        arrived(ew.at[peer], ew_send.at[0], ew_recv.at[peer])
    for step in range(n_s):
        slot = (s + step) % n_s
        wait_patch(slot, near)
        wait_patch(slot, near_far)
    embedded = jnp.zeros((img_toks, width), jnp.float32)
    for group in range(n_m):
        embedded = embedded + jnp.dot(
            patch_buf[:, group].reshape(img_toks, 4 * chan_dev),
            ew[group],
            preferred_element_type=jnp.float32,
        )
    pad = total_len - img_toks
    pad_units = pad // half
    blank = jnp.zeros((pad_units, half, width), jnp.bfloat16)
    emb_pad[0:pad_units] = blank
    emb_pad[pad_units : pad_units + n_s] = embedded.astype(jnp.bfloat16).reshape(n_s, half, width)
    emb_pad[pad_units + n_s :] = blank

    sent_hid = [0]

    def send_hid(src, slot_s, slot_m, seq, mp):
        push(
            src,
            hid_buf.at[slot_s, slot_m],
            hid_send.at[sent_hid[0]],
            hid_recv.at[slot_s, slot_m],
            seq,
            mp,
        )
        sent_hid[0] += 1

    def wait_hid(slot_s, slot_m):
        arrived(hid_buf.at[slot_s, slot_m], hid_send.at[0], hid_recv.at[slot_s, slot_m])

    per_block = tok_rows // half

    def put_block(ref, seq):
        for unit in range(per_block):
            ref[unit * half : (unit + 1) * half] = emb_pad[
                pad_units + seq * per_block + unit - start_unit
            ]

    for step in range(1, n_s):
        seq = (s + step) % n_s
        put_block(emb_out.at[seq], seq)
        send_hid(emb_out.at[seq], s, m, seq, m)
    put_block(hid_buf.at[s, m], s)
    for step in range(n_s):
        slot = (s + n_s - step) % n_s
        if step:
            wait_hid(slot, m)
        send_hid(hid_buf.at[slot, m], slot, m, s, far)
        send_hid(hid_buf.at[slot, m], slot, m, s, near)
    arrived(text_buf.at[near], text_send.at[0], text_recv.at[near])
    arrived(text_buf.at[near_far], text_send.at[0], text_recv.at[near_far])
    for copy in w_copies:
        copy.wait()
    my_pos = s * tok_rows + lax.broadcasted_iota(jnp.int32, (tok_rows, 1), 0)
    is_image = (my_pos >= start) & (my_pos < start + img_toks)
    head_cols = w_ref.shape[2]
    per_text = text_ref.shape[1] // width
    for step in range(n_s):
        slot = (s + n_s - step) % n_s
        wait_hid(slot, far)
        send_hid(hid_buf.at[slot, far], slot, far, s, near)
    for step in range(n_s):
        slot = (s + n_s - step) % n_s
        wait_hid(slot, near)
        wait_hid(slot, near_far)
        pieces = []
        for group in range(n_m):
            chunk = slot * n_m + group
            text = text_buf[
                chunk // per_text,
                :,
                pl.ds(pl.multiple_of(chunk % per_text * width, width), width),
            ]
            pieces.append(jnp.where(is_image, hid_buf[slot, group], text))
        hidden = jnp.concatenate(pieces, axis=1)
        deep = n_m * width
        for part in range(3):
            product = jnp.dot(
                hidden,
                w_buf[part, pl.ds(pl.multiple_of(slot * deep, deep), deep)],
                preferred_element_type=jnp.float32,
            )
            if step == 0:
                acc[part] = product
            else:
                acc[part] += product

    for head in range(groups):
        for part in range(3):
            qkv_out[head, :, part * HD : (part + 1) * HD] = acc[
                part, :, head * HD : (head + 1) * HD
            ].astype(jnp.bfloat16)
    sent_qkv = [0]

    def send_qkv(src, dst, slot, seq):
        push(src, dst, qkv_send.at[sent_qkv[0]], qkv_recv.at[slot], seq, m)
        sent_qkv[0] += 1

    for step in range(1, groups):
        head = (g + step) % groups
        send_qkv(qkv_out.at[head], qkv_buf.at[s], s, head * ranks + r)
    qkv_buf[s] = qkv_out[g]
    for group_step in range(groups):
        slot = (g + groups - group_step) % groups * ranks + r
        if group_step:
            arrived(qkv_buf.at[slot], qkv_send.at[0], qkv_recv.at[slot])
        kv = qkv_buf.at[slot, :, pl.ds(HD, 2 * HD)]
        for step in range(1, ranks):
            send_qkv(kv, kv, slot, g * ranks + (r + step) % ranks)
    for group_step in range(groups):
        for step in range(1, ranks):
            slot = (g + groups - group_step) % groups * ranks + (r + step) % ranks
            arrived(qkv_buf.at[slot, :, pl.ds(HD, 2 * HD)], qkv_send.at[0], qkv_recv.at[slot])

    keys = qkv_buf[:, :, HD : 2 * HD].reshape(total_len, HD)
    values = qkv_buf[:, :, 2 * HD :].reshape(total_len, HD)
    key_pos = lax.broadcasted_iota(jnp.int32, (1, total_len), 1)
    key_image = (key_pos >= start) & (key_pos < start + img_toks)
    for group_step in [*range(1, groups), 0]:
        other = (g + group_step) % groups
        slot = other * ranks + r
        query_pos = slot * tok_rows + lax.broadcasted_iota(jnp.int32, (tok_rows, 1), 0)
        query_image = (query_pos >= start) & (query_pos < start + img_toks)
        allowed = (key_pos <= query_pos) | (query_image & key_image)
        scores = (
            lax.dot_general(
                qkv_buf[slot, :, :HD],
                keys,
                (((1,), (1,)), ((), ())),
                preferred_element_type=jnp.float32,
            )
            * HD**-0.5
        )
        scores = jnp.where(allowed, scores, -1e30)
        highest = jnp.max(scores, axis=1, keepdims=True)
        weights = jnp.where(allowed, jnp.exp(scores - highest), 0.0)
        totals = jnp.sum(weights, axis=1, keepdims=True)
        result = jnp.dot(
            weights.astype(jnp.bfloat16), values, preferred_element_type=jnp.float32
        )
        result = (result / totals).astype(jnp.bfloat16)
        if group_step:
            attn_out[other] = result
            push(
                attn_out.at[other],
                attn_buf.at[g],
                attn_send.at[group_step - 1],
                attn_recv.at[g],
                slot,
                m,
            )
        else:
            attn_buf[g] = result
    for group_step in range(1, groups):
        other = (g + group_step) % groups
        arrived(attn_buf.at[other], attn_send.at[0], attn_recv.at[other])
    for head in range(groups):
        out_ref[:, head * HD : (head + 1) * HD] = attn_buf[head]

    @pl.when(s < n_s - 1)
    def _():
        edge(0, s).wait_send()

    @pl.when(s > 0)
    def _():
        edge(1, s).wait_send()

    for copy in pending:
        copy.wait_send()


def fused_shards(latents, conv_w, embed_w, text_emb, wqkv, seg_ids):
    n_s = lax.axis_size("seq")
    n_m = lax.axis_size("mp")
    tile_rows, cols, chans = latents.shape
    chan_dev = conv_w.shape[3]
    tok_rows, feats = text_emb.shape
    groups = wqkv.shape[2] // HD
    ranks = n_s // groups
    width = embed_w.shape[2] // n_m
    half = cols // 2
    total_len = seg_ids.shape[0]
    img_toks = n_s * half
    bf16 = jnp.bfloat16
    vmem = pl.BlockSpec(memory_space=pltpu.VMEM)
    dma = pltpu.SemaphoreType.DMA
    return pl.pallas_call(
        functools.partial(fused_kernel, n_s, n_m, groups),
        out_shape=jax.ShapeDtypeStruct((tok_rows, groups * HD), bf16),
        in_specs=[
            pl.BlockSpec(memory_space=pltpu.SMEM),
            vmem,
            vmem,
            vmem,
            vmem,
            pl.BlockSpec(memory_space=pl.ANY),
        ],
        out_specs=vmem,
        scratch_shapes=[
            pltpu.VMEM((3, wqkv.shape[0], wqkv.shape[2]), bf16),
            pltpu.VMEM((2, cols, chans), bf16),
            pltpu.VMEM((n_m, 4 * chan_dev, width), bf16),
            pltpu.VMEM((n_m, tok_rows, feats), bf16),
            pltpu.VMEM((n_s, n_m, half, 4 * chan_dev), bf16),
            pltpu.VMEM(((2 * total_len - img_toks) // half, half, width), bf16),
            pltpu.VMEM((n_s, tok_rows, width), bf16),
            pltpu.VMEM((n_s, n_m, tok_rows, width), bf16),
            pltpu.VMEM((3, tok_rows, wqkv.shape[2]), jnp.float32),
            pltpu.VMEM((groups, tok_rows, 3 * HD), bf16),
            pltpu.VMEM((n_s, tok_rows, 3 * HD), bf16),
            pltpu.VMEM((groups, tok_rows, HD), bf16),
            pltpu.VMEM((groups, tok_rows, HD), bf16),
            dma((3,)),
            dma((2,)),
            dma((2,)),
            dma((n_m - 1,)),
            dma((n_m,)),
            dma((3,)),
            dma((n_m,)),
            dma((groups - 1 + groups * (ranks - 1) + 3 * n_s,)),
            dma((n_s, n_m)),
            dma((n_s - 1 + 3 * n_s,)),
            dma((n_s, n_m)),
            dma((groups - 1 + groups * (ranks - 1),)),
            dma((n_s,)),
            dma((groups - 1,)),
            dma((groups,)),
        ],
        compiler_params=pltpu.CompilerParams(
            collective_id=0, has_side_effects=True, vmem_limit_bytes=48 * 1024 * 1024
        ),
        cost_estimate=pl.CostEstimate(
            flops=2 * tok_rows * wqkv.shape[0] * 3 * wqkv.shape[2],
            bytes_accessed=2 * wqkv.shape[0] * 3 * wqkv.shape[2],
            transcendentals=tok_rows * total_len * groups,
        ),
    )(
        seg_ids,
        latents,
        conv_w.transpose(0, 1, 3, 2),
        embed_w.reshape(4 * chan_dev, embed_w.shape[2]),
        text_emb,
        wqkv.transpose(1, 0, 2),
    )


def run_shards(latents, conv_w, embed_w, text_emb, wqkv, seg_ids):
    n_s = lax.axis_size("seq")
    n_m = lax.axis_size("mp")
    groups = wqkv.shape[2] // HD
    fits = n_m == 4 and n_s % groups == 0 and embed_w.shape[2] % (n_m * HD) == 0
    body = fused_shards if fits and latents.shape[0] == 2 else shards
    return body(latents, conv_w, embed_w, text_emb, wqkv, seg_ids)


def solution(mesh):
    return jax.shard_map(
        run_shards,
        mesh=mesh,
        in_specs=(
            P("seq", None, None),
            P(None, None, None, "mp"),
            P(None, "mp", "seq"),
            P("seq", "mp"),
            P(None, None, "mp"),
            P(),
        ),
        out_specs=P("seq", "mp"),
        check_vma=False,
    )
```

```python
import functools

import jax
import jax.numpy as jnp
from jax import lax
from jax.experimental import pallas as pl
from jax.experimental.pallas import tpu as pltpu
from jax.sharding import PartitionSpec as P

HD = 128


def padded_2(cells, sides, width):
    for axis, dim in sides:
        count = lax.axis_size(axis)
        ends = count - 1
        head = lax.slice_in_dim(cells, 0, width, axis=dim)
        tail = lax.slice_in_dim(cells, cells.shape[dim] - width, cells.shape[dim], axis=dim)
        cells = jnp.concatenate(
            [
                lax.ppermute(tail, axis, [(i, (i + 1) % count) for i in range(ends)]),
                cells,
                lax.ppermute(head, axis, [((i + 1) % count, i) for i in range(ends)]),
            ],
            axis=dim,
        )
    return cells


def attend_block(carry, pieces, queries, query_pos, query_seg, seg_ids, scale):
    running, totals, outputs = carry
    key_blk, value_blk = pieces
    count = key_blk.shape[0]
    heads = queries.shape[1]
    head_size = queries.shape[2]
    key_heads = key_blk.reshape(count, heads, head_size)
    value_heads = value_blk.reshape(count, heads, head_size)
    key_pos = jnp.arange(count, dtype=jnp.int32)
    allowed = (key_pos[None, :] <= query_pos[:, None]) | (
        query_seg[:, None] == seg_ids[None, :]
    ) & (query_seg[:, None] > 0)
    scores = (
        jnp.einsum("qhd,khd->hqk", queries, key_heads, preferred_element_type=jnp.float32) * scale
    )
    scores = jnp.where(allowed[None], scores, -1e30)
    updated = jnp.maximum(running, jnp.max(scores, axis=-1))
    weights = jnp.where(allowed[None], jnp.exp(scores - updated[..., None]), 0.0)
    totals = jnp.sum(weights, axis=-1)
    probs = weights.astype(jnp.bfloat16)
    outputs = jnp.einsum("hqk,khd->hqd", probs, value_heads, preferred_element_type=jnp.float32)
    return (updated, totals, outputs)


def shards(latents, conv_w, embed_w, text_emb, wqkv, seg_ids):
    tile_rows = latents.shape[0]
    tile_cols = latents.shape[1]
    channels = latents.shape[2]
    chan_dev = conv_w.shape[3]
    patch_rows = tile_rows // 2
    patch_cols = tile_cols // 2
    seq_count = lax.axis_size("seq")
    image_rows = seq_count * patch_rows
    num_images = 1
    tok_rows = text_emb.shape[0]
    total_len = seg_ids.shape[0]
    seq_index = lax.axis_index("seq")
    mp_index = lax.axis_index("mp")
    extended = padded_2(latents, (("seq", 0),), 1)
    first_row = seq_index * tile_rows
    image_height = 2 * image_rows
    keep_top = first_row % image_height != 0
    keep_bottom = (first_row + tile_rows) % image_height != 0
    row_ids = jnp.arange(tile_rows + 2, dtype=jnp.int32)
    keep = jnp.where(row_ids == 0, keep_top, jnp.where(row_ids == tile_rows + 1, keep_bottom, True))
    extended = jnp.where(keep[:, None, None], extended, jnp.zeros_like(extended))
    padded = jnp.pad(extended, ((0, 0), (1, 1), (0, 0)))
    summed = jnp.zeros((tile_rows * tile_cols, chan_dev), jnp.float32)
    for row_step in range(3):
        for col_step in range(3):
            window = padded[
                row_step : row_step + tile_rows, col_step : col_step + tile_cols, :
            ].reshape(tile_rows * tile_cols, channels)
            summed = summed + jnp.dot(
                window, conv_w[row_step, col_step], preferred_element_type=jnp.float32
            )
    own_chan = lax.dynamic_slice_in_dim(latents, mp_index * chan_dev, chan_dev, 2)
    mixed = (
        own_chan.astype(jnp.float32) + jax.nn.silu(summed.reshape(tile_rows, tile_cols, chan_dev))
    ).astype(jnp.bfloat16)
    patches = (
        mixed.reshape(patch_rows, 2, patch_cols, 2, chan_dev)
        .transpose(0, 2, 1, 3, 4)
        .reshape(patch_rows * patch_cols, 4 * chan_dev)
    )
    positions = jnp.arange(total_len, dtype=jnp.int32)
    labels = jnp.arange(1, num_images + 1, dtype=jnp.int32)
    marks = seg_ids[None, :] == labels[:, None]
    starts = jnp.min(jnp.where(marks, positions[None, :], total_len), axis=1)
    base = seq_index * tok_rows
    my_pos = base + jnp.arange(tok_rows, dtype=jnp.int32)
    piece = lax.all_gather(patches, "seq", axis=0, tiled=True)
    count = piece.shape[0]
    token = jnp.arange(count, dtype=jnp.int32)
    row_glob = token // patch_cols
    column = token % patch_cols
    image = row_glob // image_rows
    inner = row_glob % image_rows
    begin = jnp.sum(jnp.where(image[:, None] == labels[None, :] - 1, starts[None, :], 0), axis=1)
    target = begin + inner * patch_cols + column
    select = (my_pos[:, None] == target[None, :]).astype(jnp.bfloat16)
    placed = jnp.dot(select, piece, preferred_element_type=jnp.float32).astype(jnp.bfloat16)
    piece = lax.all_gather(embed_w, "seq", axis=2, tiled=True)
    partial_emb = jnp.dot(
        placed, piece.reshape(4 * chan_dev, piece.shape[2]), preferred_element_type=jnp.float32
    )
    my_seg = lax.dynamic_slice_in_dim(seg_ids, base, tok_rows, 0)
    is_text = my_seg == 0
    feat_dev = text_emb.shape[1]
    text_part = jnp.where(is_text[:, None], text_emb.astype(jnp.float32), 0.0)
    own_cols = lax.dynamic_slice_in_dim(partial_emb, mp_index * feat_dev, feat_dev, 1)
    partial_emb = lax.dynamic_update_slice_in_dim(
        partial_emb, own_cols + text_part, mp_index * feat_dev, 1
    )
    hidden = lax.psum(partial_emb, "mp").astype(jnp.bfloat16)
    width = wqkv.shape[0]
    head_cols = wqkv.shape[2]
    head_size = HD
    heads_dev = head_cols // head_size
    qkv = jnp.dot(
        hidden, wqkv.reshape(width, 3 * head_cols), preferred_element_type=jnp.float32
    ).astype(jnp.bfloat16)
    qkv = qkv.reshape(tok_rows, 3, head_cols)
    queries = qkv[:, 0].reshape(tok_rows, heads_dev, head_size)
    key_rows = qkv[:, 1]
    value_rows = qkv[:, 2]
    scale = head_size ** (-0.5)
    fold_init = (
        jnp.full((heads_dev, tok_rows), -1e30, jnp.float32),
        jnp.zeros((heads_dev, tok_rows), jnp.float32),
        jnp.zeros((heads_dev, tok_rows, head_size), jnp.float32),
    )
    running, totals, outputs = attend_block(
        fold_init,
        (
            lax.all_gather(key_rows, "seq", axis=0, tiled=True),
            lax.all_gather(value_rows, "seq", axis=0, tiled=True),
        ),
        queries,
        my_pos,
        my_seg,
        seg_ids,
        scale,
    )
    result = outputs / totals[..., None]
    return result.transpose(1, 0, 2).reshape(tok_rows, heads_dev * head_size).astype(jnp.bfloat16)


def fused_kernel(
    n_s,
    n_m,
    groups,
    seg_ref,
    lat_ref,
    conv_ref,
    embed_ref,
    text_ref,
    w_ref,
    out_ref,
    w_buf,
    lat_buf,
    conv_buf,
    halo,
    ew,
    text_buf,
    patch_out,
    patch_buf,
    emb_pad,
    emb_out,
    hid_buf,
    acc,
    qkv_out,
    qkv_buf,
    attn_out,
    attn_buf,
    load_sem,
    w_sem,
    halo_send,
    halo_recv,
    ew_send,
    ew_recv,
    text_send,
    text_recv,
    patch_send,
    far_recv,
    patch_recv,
    hid_send,
    hid_recv,
    near_recv,
    qkv_send,
    qkv_recv,
    attn_send,
    attn_recv,
):
    ranks = n_s // groups
    s = lax.axis_index("seq")
    m = lax.axis_index("mp")
    g = s // ranks
    r = s % ranks
    far = (m + 2) % n_m
    x = m // 2
    c = m % 2
    near = m + 1 - 2 * c
    near_far = (near + 2) % n_m
    cols = lat_ref.shape[1]
    chans = lat_ref.shape[2]
    chan_dev = conv_ref.shape[2]
    half = cols // 2
    tok_rows = text_ref.shape[0]
    width = ew.shape[2]
    img_toks = n_s * half
    total_len = n_s * tok_rows
    pending = []

    def my_cols(core):
        return pl.ds(pl.multiple_of(core * width, width), width)

    def push(src, dst, send, recv, seq, mp):
        copy = pltpu.make_async_remote_copy(
            src_ref=src,
            dst_ref=dst,
            send_sem=send,
            recv_sem=recv,
            device_id=(seq, mp),
            device_id_type=pl.DeviceIdType.MESH,
        )
        copy.start()
        pending.append(copy)

    def arrived(dst, send, recv):
        pltpu.make_async_remote_copy(
            src_ref=dst,
            dst_ref=dst,
            send_sem=send,
            recv_sem=recv,
            device_id=(s, near),
            device_id_type=pl.DeviceIdType.MESH,
        ).wait_recv()

    loads = [
        pltpu.make_async_copy(lat_ref, lat_buf, load_sem.at[0]),
        pltpu.make_async_copy(conv_ref, conv_buf, load_sem.at[1]),
        pltpu.make_async_copy(embed_ref.at[:, my_cols(c)], ew.at[m], load_sem.at[2]),
        pltpu.make_async_copy(text_ref, text_buf.at[m], load_sem.at[3]),
    ]
    for copy in loads:
        copy.start()
    w_copies = [
        pltpu.make_async_copy(w_ref.at[part], w_buf.at[part], w_sem.at[part]) for part in range(3)
    ]
    for copy in w_copies:
        copy.start()

    barrier = pltpu.get_barrier_semaphore()
    for step in range(1, n_s):
        pl.semaphore_signal(
            barrier, 1, device_id=((s + step) % n_s, m), device_id_type=pl.DeviceIdType.MESH
        )
    for step in range(1, n_m):
        pl.semaphore_signal(
            barrier, 1, device_id=(s, (m + step) % n_m), device_id_type=pl.DeviceIdType.MESH
        )
    pl.semaphore_wait(barrier, n_s + n_m - 2)

    def edge(first, seq):
        return pltpu.make_async_remote_copy(
            src_ref=lat_ref.at[1 - first],
            dst_ref=halo.at[first],
            send_sem=halo_send.at[first],
            recv_sem=halo_recv.at[first],
            device_id=(seq, m),
            device_id_type=pl.DeviceIdType.MESH,
        )

    @pl.when(s < n_s - 1)
    def _():
        edge(0, s + 1).start()

    @pl.when(s > 0)
    def _():
        edge(1, s - 1).start()

    for at, peer in enumerate((far, near_far, near)):
        push(
            embed_ref.at[:, my_cols(peer % 2)],
            ew.at[m],
            ew_send.at[at],
            ew_recv.at[m],
            s,
            peer,
        )

    start_unit = jnp.int32(0)
    before = jnp.int32(1)
    for unit in range((total_len - img_toks) // half):
        before = before * (1 - seg_ref[unit * half])
        start_unit = start_unit + before
    start = start_unit * half

    zero_row = jnp.zeros((cols, chans), jnp.bfloat16)

    @pl.when(s == 0)
    def _():
        halo[0] = zero_row

    @pl.when(s == n_s - 1)
    def _():
        halo[1] = zero_row

    def one_hot(rows, columns, shift):
        row = lax.broadcasted_iota(jnp.int32, (rows, columns), 0)
        column = lax.broadcasted_iota(jnp.int32, (rows, columns), 1)
        return jnp.where(column == shift(row), 1.0, 0.0).astype(jnp.bfloat16)

    picks = one_hot(4 * half, cols, lambda row: 2 * (row % half) + row // half - 1)

    def picked(row):
        return jnp.dot(picks, row, preferred_element_type=jnp.float32).astype(jnp.bfloat16)

    def taps(row, row_step):
        total = None
        for col_step in range(3):
            term = lax.dot_general(
                row[col_step * half : (col_step + 2) * half],
                conv_buf[row_step, col_step],
                (((1,), (1,)), ((), ())),
                preferred_element_type=jnp.float32,
            )
            total = term if total is None else total + term
        return total

    loads[0].wait()
    loads[1].wait()
    upper, lower = picked(lat_buf[0]), picked(lat_buf[1])
    sums = [taps(upper, 1) + taps(lower, 2), taps(upper, 0) + taps(lower, 1)]
    row = lax.broadcasted_iota(jnp.int32, (chans, chan_dev), 0)
    column = lax.broadcasted_iota(jnp.int32, (chans, chan_dev), 1)
    own = jnp.where(row == column + m * chan_dev, 1.0, 0.0).astype(jnp.bfloat16)
    own_chan = [
        jnp.dot(line[half : 3 * half], own, preferred_element_type=jnp.float32)
        for line in (upper, lower)
    ]
    places = [
        one_hot(chan_dev, 4 * chan_dev, lambda row, cell=cell: row + cell * chan_dev)
        for cell in range(4)
    ]

    @pl.when(s > 0)
    def _():
        edge(0, s).wait_recv()

    @pl.when(s < n_s - 1)
    def _():
        edge(1, s).wait_recv()

    sums = [sums[0] + taps(picked(halo[0]), 0), sums[1] + taps(picked(halo[1]), 2)]
    patches = jnp.zeros((half, 4 * chan_dev), jnp.float32)
    for line in range(2):
        mixed = (own_chan[line] + sums[line] / (1.0 + jnp.exp(-sums[line]))).astype(jnp.bfloat16)
        for side in range(2):
            patches = patches + jnp.dot(
                mixed[side * half : (side + 1) * half],
                places[2 * line + side],
                preferred_element_type=jnp.float32,
            )

    quarter = half // 2
    first_half = patches[:quarter].astype(jnp.bfloat16)
    second_half = patches[quarter:].astype(jnp.bfloat16)
    patch_buf[s, c, x] = jnp.where(x == 0, first_half, second_half)
    patch_out[...] = jnp.where(x == 0, second_half, first_half)
    push(patch_out, patch_buf.at[s, c, x], patch_send.at[0], far_recv.at[0], s, far)
    sent = [1]

    def send_patch(slot, seq, mp):
        push(
            patch_buf.at[slot, c],
            patch_buf.at[slot, c],
            patch_send.at[sent[0]],
            patch_recv.at[slot, c],
            seq,
            mp,
        )
        sent[0] += 1

    def wait_patch(slot, core):
        arrived(patch_buf.at[slot, core], patch_send.at[0], patch_recv.at[slot, core])

    arrived(patch_buf.at[s, c, 1 - x], patch_send.at[0], far_recv.at[0])
    for step in range(1, groups):
        send_patch(s, (g + step) % groups * ranks + r, m)
    for group_step in range(groups):
        slot = (g + group_step) % groups * ranks + r
        if group_step:
            wait_patch(slot, c)
        for step in range(1, ranks):
            send_patch(slot, g * ranks + (r + step) % ranks, m)
        send_patch(slot, s, near)
        if group_step == 0:
            push(text_ref, text_buf.at[m], text_send.at[0], text_recv.at[m], s, far)
            push(text_ref, text_buf.at[m], text_send.at[1], text_recv.at[m], s, near)
    for group_step in range(groups):
        for step in range(1, ranks):
            slot = (g + group_step) % groups * ranks + (r + step) % ranks
            wait_patch(slot, c)
            send_patch(slot, s, near)

    loads[2].wait()
    for peer in (far, near_far, near):
        arrived(ew.at[peer], ew_send.at[0], ew_recv.at[peer])
    for step in range(n_s):
        wait_patch((s + step) % n_s, 1 - c)
    embedded = jnp.zeros((n_s * quarter, width), jnp.float32)
    for group in range(n_m):
        embedded = embedded + jnp.dot(
            patch_buf[:, group % 2, group // 2].reshape(n_s * quarter, 4 * chan_dev),
            ew[group],
            preferred_element_type=jnp.float32,
        )
    pad_units = (total_len - img_toks) // half
    blank = jnp.zeros((pad_units, quarter, width), jnp.bfloat16)
    emb_pad[0:pad_units] = blank
    emb_pad[pad_units : pad_units + n_s] = embedded.astype(jnp.bfloat16).reshape(
        n_s, quarter, width
    )
    emb_pad[pad_units + n_s :] = blank

    per_block = tok_rows // half

    def put_block(ref, seq):
        for unit in range(per_block):
            ref[unit] = emb_pad[pad_units + seq * per_block + unit - start_unit]

    for step in range(1, n_s):
        seq = (s + step) % n_s
        put_block(emb_out.at[seq], seq)
        push(
            emb_out.at[seq],
            hid_buf.at[s, c, x],
            hid_send.at[step - 1],
            hid_recv.at[s, x],
            seq,
            m,
        )
    put_block(hid_buf.at[s, c, x], s)
    for step in range(n_s):
        slot = (s + n_s - step) % n_s
        if step:
            arrived(hid_buf.at[slot, c, x], hid_send.at[0], hid_recv.at[slot, x])
        push(
            hid_buf.at[slot, c, x],
            hid_buf.at[slot, c, x],
            hid_send.at[n_s - 1 + step],
            hid_recv.at[slot, x],
            s,
            far,
        )
    loads[3].wait()
    arrived(text_buf.at[far], text_send.at[0], text_recv.at[far])
    push(text_buf.at[far], text_buf.at[far], text_send.at[2], text_recv.at[far], s, near)
    for step in range(n_s):
        slot = (s + n_s - step) % n_s
        arrived(hid_buf.at[slot, c, 1 - x], hid_send.at[0], hid_recv.at[slot, 1 - x])
        push(
            hid_buf.at[slot, c],
            hid_buf.at[slot, c],
            hid_send.at[2 * n_s - 1 + step],
            near_recv.at[slot],
            s,
            near,
        )
    arrived(text_buf.at[near], text_send.at[0], text_recv.at[near])
    arrived(text_buf.at[near_far], text_send.at[0], text_recv.at[near_far])
    for copy in w_copies:
        copy.wait()
    my_pos = s * tok_rows + lax.broadcasted_iota(jnp.int32, (tok_rows, 1), 0)
    is_image = (my_pos >= start) & (my_pos < start + img_toks)
    per_text = text_ref.shape[1] // width
    deep = 2 * width
    for step in range(n_s):
        slot = (s + n_s - step) % n_s
        arrived(hid_buf.at[slot, 1 - c], hid_send.at[0], near_recv.at[slot])
        pieces = []
        for core in range(2):
            chunk = slot * 2 + core
            text = text_buf[
                chunk // per_text,
                :,
                pl.ds(pl.multiple_of(chunk % per_text * width, width), width),
            ]
            image = jnp.concatenate(
                [hid_buf[slot, core, side, unit] for unit in range(per_block) for side in range(2)],
                axis=0,
            )
            pieces.append(jnp.where(is_image, image, text))
        hidden = jnp.concatenate(pieces, axis=1)
        for part in range(3):
            product = jnp.dot(
                hidden,
                w_buf[part, pl.ds(pl.multiple_of(slot * deep, deep), deep)],
                preferred_element_type=jnp.float32,
            )
            if step == 0:
                acc[part] = product
            else:
                acc[part] += product

    for head in range(groups):
        for part in range(3):
            qkv_out[head, :, part * HD : (part + 1) * HD] = acc[
                part, :, head * HD : (head + 1) * HD
            ].astype(jnp.bfloat16)
    sent_qkv = [0]

    def send_qkv(src, dst, slot, seq):
        push(src, dst, qkv_send.at[sent_qkv[0]], qkv_recv.at[slot], seq, m)
        sent_qkv[0] += 1

    for step in range(1, groups):
        head = (g + step) % groups
        send_qkv(qkv_out.at[head], qkv_buf.at[s], s, head * ranks + r)
    qkv_buf[s] = qkv_out[g]
    for group_step in range(groups):
        slot = (g + groups - group_step) % groups * ranks + r
        if group_step:
            arrived(qkv_buf.at[slot], qkv_send.at[0], qkv_recv.at[slot])
        kv = qkv_buf.at[slot, :, pl.ds(HD, 2 * HD)]
        for step in range(1, ranks):
            send_qkv(kv, kv, slot, g * ranks + (r + step) % ranks)
    for group_step in range(groups):
        for step in range(1, ranks):
            slot = (g + groups - group_step) % groups * ranks + (r + step) % ranks
            arrived(qkv_buf.at[slot, :, pl.ds(HD, 2 * HD)], qkv_send.at[0], qkv_recv.at[slot])

    keys = qkv_buf[:, :, HD : 2 * HD].reshape(total_len, HD)
    values = qkv_buf[:, :, 2 * HD :].reshape(total_len, HD)
    key_pos = lax.broadcasted_iota(jnp.int32, (1, total_len), 1)
    key_image = (key_pos >= start) & (key_pos < start + img_toks)
    for group_step in [*range(1, groups), 0]:
        other = (g + group_step) % groups
        slot = other * ranks + r
        query_pos = slot * tok_rows + lax.broadcasted_iota(jnp.int32, (tok_rows, 1), 0)
        query_image = (query_pos >= start) & (query_pos < start + img_toks)
        allowed = (key_pos <= query_pos) | (query_image & key_image)
        scores = (
            lax.dot_general(
                qkv_buf[slot, :, :HD],
                keys,
                (((1,), (1,)), ((), ())),
                preferred_element_type=jnp.float32,
            )
            * HD**-0.5
        )
        scores = jnp.where(allowed, scores, -1e30)
        highest = jnp.max(scores, axis=1, keepdims=True)
        weights = jnp.where(allowed, jnp.exp(scores - highest), 0.0)
        totals = jnp.sum(weights, axis=1, keepdims=True)
        result = jnp.dot(
            weights.astype(jnp.bfloat16), values, preferred_element_type=jnp.float32
        )
        result = (result / totals).astype(jnp.bfloat16)
        if group_step:
            attn_out[other] = result
            push(
                attn_out.at[other],
                attn_buf.at[g],
                attn_send.at[group_step - 1],
                attn_recv.at[g],
                slot,
                m,
            )
        else:
            attn_buf[g] = result
    for group_step in range(1, groups):
        other = (g + group_step) % groups
        arrived(attn_buf.at[other], attn_send.at[0], attn_recv.at[other])
    for head in range(groups):
        out_ref[:, head * HD : (head + 1) * HD] = attn_buf[head]

    @pl.when(s < n_s - 1)
    def _():
        edge(0, s).wait_send()

    @pl.when(s > 0)
    def _():
        edge(1, s).wait_send()

    for copy in pending:
        copy.wait_send()


def fused_shards(latents, conv_w, embed_w, text_emb, wqkv, seg_ids):
    n_s = lax.axis_size("seq")
    n_m = lax.axis_size("mp")
    tile_rows, cols, chans = latents.shape
    chan_dev = conv_w.shape[3]
    tok_rows, feats = text_emb.shape
    groups = wqkv.shape[2] // HD
    ranks = n_s // groups
    width = embed_w.shape[2] // 2
    half = cols // 2
    total_len = seg_ids.shape[0]
    img_toks = n_s * half
    bf16 = jnp.bfloat16
    vmem = pl.BlockSpec(memory_space=pltpu.VMEM)
    hbm = pl.BlockSpec(memory_space=pltpu.HBM)
    dma = pltpu.SemaphoreType.DMA
    return pl.pallas_call(
        functools.partial(fused_kernel, n_s, n_m, groups),
        out_shape=jax.ShapeDtypeStruct((tok_rows, groups * HD), bf16),
        in_specs=[
            pl.BlockSpec(memory_space=pltpu.SMEM),
            hbm,
            hbm,
            hbm,
            hbm,
            hbm,
        ],
        out_specs=vmem,
        scratch_shapes=[
            pltpu.VMEM((3, wqkv.shape[0], wqkv.shape[2]), bf16),
            pltpu.VMEM((2, cols, chans), bf16),
            pltpu.VMEM((3, 3, chan_dev, chans), bf16),
            pltpu.VMEM((2, cols, chans), bf16),
            pltpu.VMEM((n_m, 4 * chan_dev, width), bf16),
            pltpu.VMEM((n_m, tok_rows, feats), bf16),
            pltpu.VMEM((half // 2, 4 * chan_dev), bf16),
            pltpu.VMEM((n_s, 2, 2, half // 2, 4 * chan_dev), bf16),
            pltpu.VMEM(((2 * total_len - img_toks) // half, half // 2, width), bf16),
            pltpu.VMEM((n_s, tok_rows // half, half // 2, width), bf16),
            pltpu.VMEM((n_s, 2, 2, tok_rows // half, half // 2, width), bf16),
            pltpu.VMEM((3, tok_rows, wqkv.shape[2]), jnp.float32),
            pltpu.VMEM((groups, tok_rows, 3 * HD), bf16),
            pltpu.VMEM((n_s, tok_rows, 3 * HD), bf16),
            pltpu.VMEM((groups, tok_rows, HD), bf16),
            pltpu.VMEM((groups, tok_rows, HD), bf16),
            dma((4,)),
            dma((3,)),
            dma((2,)),
            dma((2,)),
            dma((n_m - 1,)),
            dma((n_m,)),
            dma((3,)),
            dma((n_m,)),
            dma((1 + groups - 1 + groups * (ranks - 1) + n_s,)),
            dma((1,)),
            dma((n_s, 2)),
            dma((n_s - 1 + 2 * n_s,)),
            dma((n_s, 2)),
            dma((n_s,)),
            dma((groups - 1 + groups * (ranks - 1),)),
            dma((n_s,)),
            dma((groups - 1,)),
            dma((groups,)),
        ],
        compiler_params=pltpu.CompilerParams(
            collective_id=0, has_side_effects=True, vmem_limit_bytes=60 * 1024 * 1024
        ),
        cost_estimate=pl.CostEstimate(
            flops=2 * tok_rows * wqkv.shape[0] * 3 * wqkv.shape[2],
            bytes_accessed=2 * wqkv.shape[0] * 3 * wqkv.shape[2],
            transcendentals=tok_rows * total_len * groups,
        ),
    )(
        seg_ids,
        latents,
        conv_w.transpose(0, 1, 3, 2),
        embed_w.reshape(4 * chan_dev, embed_w.shape[2]),
        text_emb,
        wqkv.transpose(1, 0, 2),
    )


def run_shards(latents, conv_w, embed_w, text_emb, wqkv, seg_ids):
    n_s = lax.axis_size("seq")
    n_m = lax.axis_size("mp")
    groups = wqkv.shape[2] // HD
    fits = n_m == 4 and n_s % groups == 0 and embed_w.shape[2] % (2 * HD) == 0
    body = fused_shards if fits and latents.shape[0] == 2 else shards
    return body(latents, conv_w, embed_w, text_emb, wqkv, seg_ids)


def solution(mesh):
    return jax.shard_map(
        run_shards,
        mesh=mesh,
        in_specs=(
            P("seq", None, None),
            P(None, None, None, "mp"),
            P(None, "mp", "seq"),
            P("seq", "mp"),
            P(None, None, "mp"),
            P(),
        ),
        out_specs=P("seq", "mp"),
        check_vma=False,
    )
```

```python
import functools
import math

import jax
import jax.numpy as jnp
from jax import lax
from jax.experimental import pallas as pl
from jax.experimental.pallas import tpu as pltpu
from jax.sharding import PartitionSpec as P

HD = 128


def padded_2(cells, sides, width):
    for axis, dim in sides:
        count = lax.axis_size(axis)
        ends = count - 1
        head = lax.slice_in_dim(cells, 0, width, axis=dim)
        tail = lax.slice_in_dim(cells, cells.shape[dim] - width, cells.shape[dim], axis=dim)
        cells = jnp.concatenate(
            [
                lax.ppermute(tail, axis, [(i, (i + 1) % count) for i in range(ends)]),
                cells,
                lax.ppermute(head, axis, [((i + 1) % count, i) for i in range(ends)]),
            ],
            axis=dim,
        )
    return cells


def attend_block(carry, pieces, queries, query_pos, query_seg, seg_ids, scale):
    running, totals, outputs = carry
    key_blk, value_blk = pieces
    count = key_blk.shape[0]
    heads = queries.shape[1]
    head_size = queries.shape[2]
    key_heads = key_blk.reshape(count, heads, head_size)
    value_heads = value_blk.reshape(count, heads, head_size)
    key_pos = jnp.arange(count, dtype=jnp.int32)
    allowed = (key_pos[None, :] <= query_pos[:, None]) | (
        query_seg[:, None] == seg_ids[None, :]
    ) & (query_seg[:, None] > 0)
    scores = (
        jnp.einsum("qhd,khd->hqk", queries, key_heads, preferred_element_type=jnp.float32) * scale
    )
    scores = jnp.where(allowed[None], scores, -1e30)
    updated = jnp.maximum(running, jnp.max(scores, axis=-1))
    weights = jnp.where(allowed[None], jnp.exp(scores - updated[..., None]), 0.0)
    totals = jnp.sum(weights, axis=-1)
    probs = weights.astype(jnp.bfloat16)
    outputs = jnp.einsum("hqk,khd->hqd", probs, value_heads, preferred_element_type=jnp.float32)
    return (updated, totals, outputs)


def shards(latents, conv_w, embed_w, text_emb, wqkv, seg_ids):
    tile_rows = latents.shape[0]
    tile_cols = latents.shape[1]
    channels = latents.shape[2]
    chan_dev = conv_w.shape[3]
    patch_rows = tile_rows // 2
    patch_cols = tile_cols // 2
    seq_count = lax.axis_size("seq")
    image_rows = seq_count * patch_rows
    num_images = 1
    tok_rows = text_emb.shape[0]
    total_len = seg_ids.shape[0]
    seq_index = lax.axis_index("seq")
    mp_index = lax.axis_index("mp")
    extended = padded_2(latents, (("seq", 0),), 1)
    first_row = seq_index * tile_rows
    image_height = 2 * image_rows
    keep_top = first_row % image_height != 0
    keep_bottom = (first_row + tile_rows) % image_height != 0
    row_ids = jnp.arange(tile_rows + 2, dtype=jnp.int32)
    keep = jnp.where(row_ids == 0, keep_top, jnp.where(row_ids == tile_rows + 1, keep_bottom, True))
    extended = jnp.where(keep[:, None, None], extended, jnp.zeros_like(extended))
    padded = jnp.pad(extended, ((0, 0), (1, 1), (0, 0)))
    summed = jnp.zeros((tile_rows * tile_cols, chan_dev), jnp.float32)
    for row_step in range(3):
        for col_step in range(3):
            window = padded[
                row_step : row_step + tile_rows, col_step : col_step + tile_cols, :
            ].reshape(tile_rows * tile_cols, channels)
            summed = summed + jnp.dot(
                window, conv_w[row_step, col_step], preferred_element_type=jnp.float32
            )
    own_chan = lax.dynamic_slice_in_dim(latents, mp_index * chan_dev, chan_dev, 2)
    mixed = (
        own_chan.astype(jnp.float32) + jax.nn.silu(summed.reshape(tile_rows, tile_cols, chan_dev))
    ).astype(jnp.bfloat16)
    patches = (
        mixed.reshape(patch_rows, 2, patch_cols, 2, chan_dev)
        .transpose(0, 2, 1, 3, 4)
        .reshape(patch_rows * patch_cols, 4 * chan_dev)
    )
    positions = jnp.arange(total_len, dtype=jnp.int32)
    labels = jnp.arange(1, num_images + 1, dtype=jnp.int32)
    marks = seg_ids[None, :] == labels[:, None]
    starts = jnp.min(jnp.where(marks, positions[None, :], total_len), axis=1)
    base = seq_index * tok_rows
    my_pos = base + jnp.arange(tok_rows, dtype=jnp.int32)
    piece = lax.all_gather(patches, "seq", axis=0, tiled=True)
    count = piece.shape[0]
    token = jnp.arange(count, dtype=jnp.int32)
    row_glob = token // patch_cols
    column = token % patch_cols
    image = row_glob // image_rows
    inner = row_glob % image_rows
    begin = jnp.sum(jnp.where(image[:, None] == labels[None, :] - 1, starts[None, :], 0), axis=1)
    target = begin + inner * patch_cols + column
    select = (my_pos[:, None] == target[None, :]).astype(jnp.bfloat16)
    placed = jnp.dot(select, piece, preferred_element_type=jnp.float32).astype(jnp.bfloat16)
    piece = lax.all_gather(embed_w, "seq", axis=2, tiled=True)
    partial_emb = jnp.dot(
        placed, piece.reshape(4 * chan_dev, piece.shape[2]), preferred_element_type=jnp.float32
    )
    my_seg = lax.dynamic_slice_in_dim(seg_ids, base, tok_rows, 0)
    is_text = my_seg == 0
    feat_dev = text_emb.shape[1]
    text_part = jnp.where(is_text[:, None], text_emb.astype(jnp.float32), 0.0)
    own_cols = lax.dynamic_slice_in_dim(partial_emb, mp_index * feat_dev, feat_dev, 1)
    partial_emb = lax.dynamic_update_slice_in_dim(
        partial_emb, own_cols + text_part, mp_index * feat_dev, 1
    )
    hidden = lax.psum(partial_emb, "mp").astype(jnp.bfloat16)
    width = wqkv.shape[0]
    head_cols = wqkv.shape[2]
    head_size = HD
    heads_dev = head_cols // head_size
    qkv = jnp.dot(
        hidden, wqkv.reshape(width, 3 * head_cols), preferred_element_type=jnp.float32
    ).astype(jnp.bfloat16)
    qkv = qkv.reshape(tok_rows, 3, head_cols)
    queries = qkv[:, 0].reshape(tok_rows, heads_dev, head_size)
    key_rows = qkv[:, 1]
    value_rows = qkv[:, 2]
    scale = head_size ** (-0.5)
    fold_init = (
        jnp.full((heads_dev, tok_rows), -1e30, jnp.float32),
        jnp.zeros((heads_dev, tok_rows), jnp.float32),
        jnp.zeros((heads_dev, tok_rows, head_size), jnp.float32),
    )
    running, totals, outputs = attend_block(
        fold_init,
        (
            lax.all_gather(key_rows, "seq", axis=0, tiled=True),
            lax.all_gather(value_rows, "seq", axis=0, tiled=True),
        ),
        queries,
        my_pos,
        my_seg,
        seg_ids,
        scale,
    )
    result = outputs / totals[..., None]
    return result.transpose(1, 0, 2).reshape(tok_rows, heads_dev * head_size).astype(jnp.bfloat16)


def fused_kernel(
    n_s,
    n_m,
    groups,
    seg_ref,
    lat_ref,
    conv_ref,
    embed_ref,
    text_ref,
    w_ref,
    out_ref,
    w_buf,
    lat_buf,
    conv_buf,
    halo,
    ew,
    text_buf,
    patch_out,
    patch_buf,
    emb_pad,
    emb_out,
    hid_buf,
    acc,
    qkv_out,
    qkv_buf,
    score_buf,
    prob_buf,
    attn_out,
    attn_buf,
    load_sem,
    w_sem,
    halo_send,
    halo_recv,
    ew_send,
    ew_recv,
    text_send,
    text_recv,
    patch_send,
    far_recv,
    patch_recv,
    hid_send,
    hid_recv,
    near_recv,
    qkv_send,
    qkv_recv,
    query_send,
    query_recv,
    attn_send,
    attn_recv,
):
    ranks = n_s // groups
    s = lax.axis_index("seq")
    m = lax.axis_index("mp")
    g = s // ranks
    r = s % ranks
    far = (m + 2) % n_m
    x = m // 2
    c = m % 2
    near = m + 1 - 2 * c
    near_far = (near + 2) % n_m
    cols = lat_ref.shape[1]
    chans = lat_ref.shape[2]
    chan_dev = conv_ref.shape[2]
    half = cols // 2
    tok_rows = text_ref.shape[0]
    width = ew.shape[2]
    img_toks = n_s * half
    total_len = n_s * tok_rows
    pending = []

    def my_cols(core):
        return pl.ds(pl.multiple_of(core * width, width), width)

    def push(src, dst, send, recv, seq, mp):
        copy = pltpu.make_async_remote_copy(
            src_ref=src,
            dst_ref=dst,
            send_sem=send,
            recv_sem=recv,
            device_id=(seq, mp),
            device_id_type=pl.DeviceIdType.MESH,
        )
        copy.start()
        pending.append(copy)

    def arrived(dst, send, recv):
        pltpu.make_async_remote_copy(
            src_ref=dst,
            dst_ref=dst,
            send_sem=send,
            recv_sem=recv,
            device_id=(s, near),
            device_id_type=pl.DeviceIdType.MESH,
        ).wait_recv()

    loads = [
        pltpu.make_async_copy(lat_ref, lat_buf, load_sem.at[0]),
        pltpu.make_async_copy(conv_ref, conv_buf, load_sem.at[1]),
        pltpu.make_async_copy(embed_ref.at[:, my_cols(c)], ew.at[m], load_sem.at[2]),
        pltpu.make_async_copy(text_ref, text_buf.at[m], load_sem.at[3]),
    ]
    for copy in loads:
        copy.start()
    barrier = pltpu.get_barrier_semaphore()
    for step in range(1, n_s):
        pl.semaphore_signal(
            barrier, 1, device_id=((s + step) % n_s, m), device_id_type=pl.DeviceIdType.MESH
        )
    for step in range(1, n_m):
        pl.semaphore_signal(
            barrier, 1, device_id=(s, (m + step) % n_m), device_id_type=pl.DeviceIdType.MESH
        )
    pl.semaphore_wait(barrier, n_s + n_m - 2)

    loads[0].wait()

    def edge(first, seq):
        return pltpu.make_async_remote_copy(
            src_ref=lat_buf.at[1 - first],
            dst_ref=halo.at[first],
            send_sem=halo_send.at[first],
            recv_sem=halo_recv.at[first],
            device_id=(seq, m),
            device_id_type=pl.DeviceIdType.MESH,
        )

    @pl.when(s < n_s - 1)
    def _():
        edge(0, s + 1).start()

    @pl.when(s > 0)
    def _():
        edge(1, s - 1).start()

    for at, peer in enumerate((far, near_far, near)):
        push(
            embed_ref.at[:, my_cols(peer % 2)],
            ew.at[m],
            ew_send.at[at],
            ew_recv.at[m],
            s,
            peer,
        )

    start_unit = jnp.int32(0)
    before = jnp.int32(1)
    for unit in range((total_len - img_toks) // half):
        before = before * (1 - seg_ref[unit * half])
        start_unit = start_unit + before
    start = start_unit * half

    zero_row = jnp.zeros((cols, chans), jnp.bfloat16)

    @pl.when(s == 0)
    def _():
        halo[0] = zero_row

    @pl.when(s == n_s - 1)
    def _():
        halo[1] = zero_row

    def one_hot(rows, columns, shift):
        row = lax.broadcasted_iota(jnp.int32, (rows, columns), 0)
        column = lax.broadcasted_iota(jnp.int32, (rows, columns), 1)
        return jnp.where(column == shift(row), 1.0, 0.0).astype(jnp.bfloat16)

    picks = one_hot(4 * half, cols, lambda row: 2 * (row % half) + row // half - 1)

    def picked(row):
        return jnp.dot(picks, row, preferred_element_type=jnp.float32).astype(jnp.bfloat16)

    def taps(row, row_step):
        total = None
        for col_step in range(3):
            term = lax.dot_general(
                row[col_step * half : (col_step + 2) * half],
                conv_buf[row_step, col_step],
                (((1,), (1,)), ((), ())),
                preferred_element_type=jnp.float32,
            )
            total = term if total is None else total + term
        return total

    loads[1].wait()
    upper, lower = picked(lat_buf[0]), picked(lat_buf[1])
    sums = [taps(upper, 1) + taps(lower, 2), taps(upper, 0) + taps(lower, 1)]
    row = lax.broadcasted_iota(jnp.int32, (chans, chan_dev), 0)
    column = lax.broadcasted_iota(jnp.int32, (chans, chan_dev), 1)
    own = jnp.where(row == column + m * chan_dev, 1.0, 0.0).astype(jnp.bfloat16)
    own_chan = [
        jnp.dot(line[half : 3 * half], own, preferred_element_type=jnp.float32)
        for line in (upper, lower)
    ]
    places = [
        one_hot(chan_dev, 4 * chan_dev, lambda row, cell=cell: row + cell * chan_dev)
        for cell in range(4)
    ]

    @pl.when(s > 0)
    def _():
        edge(0, s).wait_recv()

    @pl.when(s < n_s - 1)
    def _():
        edge(1, s).wait_recv()

    sums = [sums[0] + taps(picked(halo[0]), 0), sums[1] + taps(picked(halo[1]), 2)]
    patches = jnp.zeros((half, 4 * chan_dev), jnp.float32)
    for line in range(2):
        mixed = (own_chan[line] + sums[line] / (1.0 + jnp.exp(-sums[line]))).astype(jnp.bfloat16)
        for side in range(2):
            patches = patches + jnp.dot(
                mixed[side * half : (side + 1) * half],
                places[2 * line + side],
                preferred_element_type=jnp.float32,
            )

    quarter = half // 2
    first_half = patches[:quarter].astype(jnp.bfloat16)
    second_half = patches[quarter:].astype(jnp.bfloat16)
    patch_buf[s, c, x] = jnp.where(x == 0, first_half, second_half)
    patch_out[...] = jnp.where(x == 0, second_half, first_half)
    push(patch_out, patch_buf.at[s, c, x], patch_send.at[0], far_recv.at[0], s, far)
    w_copies = [
        pltpu.make_async_copy(w_ref.at[part], w_buf.at[part], w_sem.at[part]) for part in range(3)
    ]
    for copy in w_copies:
        copy.start()

    sent = [1]

    def send_patch(slot, seq, mp):
        push(
            patch_buf.at[slot, c],
            patch_buf.at[slot, c],
            patch_send.at[sent[0]],
            patch_recv.at[slot, c],
            seq,
            mp,
        )
        sent[0] += 1

    def wait_patch(slot, core):
        arrived(patch_buf.at[slot, core], patch_send.at[0], patch_recv.at[slot, core])

    arrived(patch_buf.at[s, c, 1 - x], patch_send.at[0], far_recv.at[0])
    for step in range(1, groups):
        send_patch(s, (g + step) % groups * ranks + r, m)
    for group_step in range(groups):
        slot = (g + group_step) % groups * ranks + r
        if group_step:
            wait_patch(slot, c)
        for step in range(1, ranks):
            send_patch(slot, g * ranks + (r + step) % ranks, m)
        send_patch(slot, s, near)
        if group_step == 0:
            push(text_ref, text_buf.at[m], text_send.at[0], text_recv.at[m], s, far)
            push(text_ref, text_buf.at[m], text_send.at[1], text_recv.at[m], s, near)
    for group_step in range(groups):
        for step in range(1, ranks):
            slot = (g + group_step) % groups * ranks + (r + step) % ranks
            wait_patch(slot, c)
            send_patch(slot, s, near)

    loads[2].wait()
    for peer in (far, near_far, near):
        arrived(ew.at[peer], ew_send.at[0], ew_recv.at[peer])
    for step in range(n_s):
        wait_patch((s + step) % n_s, 1 - c)
    embedded = jnp.zeros((n_s * quarter, width), jnp.float32)
    for group in range(n_m):
        embedded = embedded + jnp.dot(
            patch_buf[:, group % 2, group // 2].reshape(n_s * quarter, 4 * chan_dev),
            ew[group],
            preferred_element_type=jnp.float32,
        )
    pad_units = (total_len - img_toks) // half
    blank = jnp.zeros((pad_units, quarter, width), jnp.bfloat16)
    emb_pad[0:pad_units] = blank
    emb_pad[pad_units : pad_units + n_s] = embedded.astype(jnp.bfloat16).reshape(
        n_s, quarter, width
    )
    emb_pad[pad_units + n_s :] = blank

    per_block = tok_rows // half

    def put_block(ref, seq):
        for unit in range(per_block):
            ref[unit] = emb_pad[pad_units + seq * per_block + unit - start_unit]

    for step in range(1, n_s):
        seq = (s + step) % n_s
        put_block(emb_out.at[seq], seq)
        push(
            emb_out.at[seq],
            hid_buf.at[s, c, x],
            hid_send.at[step - 1],
            hid_recv.at[s, x],
            seq,
            m,
        )
    put_block(hid_buf.at[s, c, x], s)
    for step in range(n_s):
        slot = (s + n_s - step) % n_s
        if step:
            arrived(hid_buf.at[slot, c, x], hid_send.at[0], hid_recv.at[slot, x])
        push(
            hid_buf.at[slot, c, x],
            hid_buf.at[slot, c, x],
            hid_send.at[n_s - 1 + step],
            hid_recv.at[slot, x],
            s,
            far,
        )
    loads[3].wait()
    arrived(text_buf.at[far], text_send.at[0], text_recv.at[far])
    push(text_buf.at[far], text_buf.at[far], text_send.at[2], text_recv.at[far], s, near)
    for step in range(n_s):
        slot = (s + n_s - step) % n_s
        arrived(hid_buf.at[slot, c, 1 - x], hid_send.at[0], hid_recv.at[slot, 1 - x])
        push(
            hid_buf.at[slot, c],
            hid_buf.at[slot, c],
            hid_send.at[2 * n_s - 1 + step],
            near_recv.at[slot],
            s,
            near,
        )
    arrived(text_buf.at[near], text_send.at[0], text_recv.at[near])
    arrived(text_buf.at[near_far], text_send.at[0], text_recv.at[near_far])
    for copy in w_copies:
        copy.wait()
    my_pos = s * tok_rows + lax.broadcasted_iota(jnp.int32, (tok_rows, 1), 0)
    is_image = (my_pos >= start) & (my_pos < start + img_toks)
    per_text = text_ref.shape[1] // width
    deep = 2 * width
    for step in range(n_s):
        slot = (s + n_s - step) % n_s
        arrived(hid_buf.at[slot, 1 - c], hid_send.at[0], near_recv.at[slot])
        pieces = []
        for core in range(2):
            chunk = slot * 2 + core
            text = text_buf[
                chunk // per_text,
                :,
                pl.ds(pl.multiple_of(chunk % per_text * width, width), width),
            ]
            image = jnp.concatenate(
                [hid_buf[slot, core, side, unit] for unit in range(per_block) for side in range(2)],
                axis=0,
            )
            pieces.append(jnp.where(is_image, image, text))
        hidden = jnp.concatenate(pieces, axis=1)
        for part in range(3):
            product = jnp.dot(
                hidden,
                w_buf[part, pl.ds(pl.multiple_of(slot * deep, deep), deep)],
                preferred_element_type=jnp.float32,
            )
            if step == 0:
                acc[part] = product
            else:
                acc[part] += product

    for head in range(groups):
        for part in range(3):
            qkv_out[head, :, part * HD : (part + 1) * HD] = acc[
                part, :, head * HD : (head + 1) * HD
            ].astype(jnp.bfloat16)
    sent_qkv = [0]

    def send_qkv(src, dst, slot, seq):
        push(src, dst, qkv_send.at[sent_qkv[0]], qkv_recv.at[slot], seq, m)
        sent_qkv[0] += 1

    key_cols = pl.ds(HD, 2 * HD)
    query_cols = pl.ds(0, HD)
    for step in range(1, groups):
        head = (g + step) % groups
        send_qkv(
            qkv_out.at[head, :, key_cols], qkv_buf.at[s, :, key_cols], s, head * ranks + r
        )
    qkv_buf[s] = qkv_out[g]
    for step in range(1, ranks):
        kv = qkv_buf.at[s, :, key_cols]
        send_qkv(kv, kv, s, g * ranks + (r + step) % ranks)
    for step in range(1, groups):
        head = (g + step) % groups
        push(
            qkv_out.at[head, :, query_cols],
            qkv_buf.at[s, :, query_cols],
            query_send.at[step - 1],
            query_recv.at[s],
            head * ranks + r,
            m,
        )
    for group_step in range(1, groups):
        slot = (g + groups - group_step) % groups * ranks + r
        kv = qkv_buf.at[slot, :, key_cols]
        arrived(kv, qkv_send.at[0], qkv_recv.at[slot])
        for step in range(1, ranks):
            send_qkv(kv, kv, slot, g * ranks + (r + step) % ranks)

    done = len(pending) - groups * ranks - groups
    for copy in pending[:done]:
        copy.wait_send()
    del pending[:done]

    @pl.when(s < n_s - 1)
    def _():
        edge(0, s).wait_send()

    @pl.when(s > 0)
    def _():
        edge(1, s).wait_send()

    for group_step in range(1, groups):
        slot = (g + groups - group_step) % groups * ranks + r
        arrived(qkv_buf.at[slot, :, query_cols], query_send.at[0], query_recv.at[slot])
    for group_step in range(groups):
        for step in range(1, ranks):
            slot = (g + groups - group_step) % groups * ranks + (r + step) % ranks
            arrived(qkv_buf.at[slot, :, key_cols], qkv_send.at[0], qkv_recv.at[slot])

    keys = qkv_buf[:, :, HD : 2 * HD].reshape(total_len, HD)
    values = qkv_buf[:, :, 2 * HD :].reshape(total_len, HD)
    order = [*range(1, groups), 0]
    queries = jnp.concatenate(
        [qkv_buf[(g + step) % groups * ranks + r, :, :HD] for step in order], axis=0
    )
    score_buf[...] = lax.dot_general(
        queries, keys, (((1,), (1,)), ((), ())), preferred_element_type=jnp.float32
    )
    tile = min(32, tok_rows)
    key_pos = lax.broadcasted_iota(jnp.int32, (tile, total_len), 1)
    for at, group_step in enumerate(order):
        other = (g + group_step) % groups
        slot = other * ranks + r
        totals = []
        for row in range(0, tok_rows, tile):
            query_pos = slot * tok_rows + row + lax.broadcasted_iota(jnp.int32, (tile, 1), 0)
            query_image = (query_pos >= start) & (query_pos < start + img_toks)
            last_seen = jnp.where(query_image, start + img_toks - 1, query_pos)
            scores = score_buf[at * tok_rows + row : at * tok_rows + row + tile]
            scores = jnp.where(key_pos <= last_seen, scores, -1e30)
            highest = jnp.max(scores, axis=1, keepdims=True)
            weights = jnp.exp2((scores - highest) * (HD**-0.5 * math.log2(math.e)))
            totals.append(jnp.sum(weights, axis=1, keepdims=True))
            prob_buf[row : row + tile] = weights.astype(jnp.bfloat16)
        result = jnp.dot(prob_buf[...], values, preferred_element_type=jnp.float32)
        result = (result / jnp.concatenate(totals, axis=0)).astype(jnp.bfloat16)
        if group_step:
            attn_out[other] = result
            push(
                attn_out.at[other],
                attn_buf.at[g],
                attn_send.at[group_step - 1],
                attn_recv.at[g],
                slot,
                m,
            )
        else:
            attn_buf[g] = result
    for group_step in range(1, groups):
        other = (g + group_step) % groups
        arrived(attn_buf.at[other], attn_send.at[0], attn_recv.at[other])
    for head in range(groups):
        out_ref[:, head * HD : (head + 1) * HD] = attn_buf[head]
    for copy in pending:
        copy.wait_send()


def fused_shards(latents, conv_w, embed_w, text_emb, wqkv, seg_ids):
    n_s = lax.axis_size("seq")
    n_m = lax.axis_size("mp")
    tile_rows, cols, chans = latents.shape
    chan_dev = conv_w.shape[3]
    tok_rows, feats = text_emb.shape
    groups = wqkv.shape[2] // HD
    ranks = n_s // groups
    width = embed_w.shape[2] // 2
    half = cols // 2
    total_len = seg_ids.shape[0]
    img_toks = n_s * half
    bf16 = jnp.bfloat16
    vmem = pl.BlockSpec(memory_space=pltpu.VMEM)
    hbm = pl.BlockSpec(memory_space=pltpu.HBM)
    dma = pltpu.SemaphoreType.DMA
    return pl.pallas_call(
        functools.partial(fused_kernel, n_s, n_m, groups),
        out_shape=jax.ShapeDtypeStruct((tok_rows, groups * HD), bf16),
        in_specs=[
            pl.BlockSpec(memory_space=pltpu.SMEM),
            hbm,
            hbm,
            hbm,
            hbm,
            hbm,
        ],
        out_specs=vmem,
        scratch_shapes=[
            pltpu.VMEM((3, wqkv.shape[0], wqkv.shape[2]), bf16),
            pltpu.VMEM((2, cols, chans), bf16),
            pltpu.VMEM((3, 3, chan_dev, chans), bf16),
            pltpu.VMEM((2, cols, chans), bf16),
            pltpu.VMEM((n_m, 4 * chan_dev, width), bf16),
            pltpu.VMEM((n_m, tok_rows, feats), bf16),
            pltpu.VMEM((half // 2, 4 * chan_dev), bf16),
            pltpu.VMEM((n_s, 2, 2, half // 2, 4 * chan_dev), bf16),
            pltpu.VMEM(((2 * total_len - img_toks) // half, half // 2, width), bf16),
            pltpu.VMEM((n_s, tok_rows // half, half // 2, width), bf16),
            pltpu.VMEM((n_s, 2, 2, tok_rows // half, half // 2, width), bf16),
            pltpu.VMEM((3, tok_rows, wqkv.shape[2]), jnp.float32),
            pltpu.VMEM((groups, tok_rows, 3 * HD), bf16),
            pltpu.VMEM((n_s, tok_rows, 3 * HD), bf16),
            pltpu.VMEM((groups * tok_rows, total_len), jnp.float32),
            pltpu.VMEM((tok_rows, total_len), bf16),
            pltpu.VMEM((groups, tok_rows, HD), bf16),
            pltpu.VMEM((groups, tok_rows, HD), bf16),
            dma((4,)),
            dma((3,)),
            dma((2,)),
            dma((2,)),
            dma((n_m - 1,)),
            dma((n_m,)),
            dma((3,)),
            dma((n_m,)),
            dma((1 + groups - 1 + groups * (ranks - 1) + n_s,)),
            dma((1,)),
            dma((n_s, 2)),
            dma((n_s - 1 + 2 * n_s,)),
            dma((n_s, 2)),
            dma((n_s,)),
            dma((groups - 1 + groups * (ranks - 1),)),
            dma((n_s,)),
            dma((groups - 1,)),
            dma((n_s,)),
            dma((groups - 1,)),
            dma((groups,)),
        ],
        compiler_params=pltpu.CompilerParams(
            collective_id=0, has_side_effects=True, vmem_limit_bytes=60 * 1024 * 1024
        ),
        cost_estimate=pl.CostEstimate(
            flops=2 * tok_rows * wqkv.shape[0] * 3 * wqkv.shape[2],
            bytes_accessed=2 * wqkv.shape[0] * 3 * wqkv.shape[2],
            transcendentals=tok_rows * total_len * groups,
        ),
    )(
        seg_ids,
        latents,
        conv_w.transpose(0, 1, 3, 2),
        embed_w.reshape(4 * chan_dev, embed_w.shape[2]),
        text_emb,
        wqkv.transpose(1, 0, 2),
    )


def run_shards(latents, conv_w, embed_w, text_emb, wqkv, seg_ids):
    n_s = lax.axis_size("seq")
    n_m = lax.axis_size("mp")
    groups = wqkv.shape[2] // HD
    fits = n_m == 4 and n_s % groups == 0 and embed_w.shape[2] % (2 * HD) == 0
    body = fused_shards if fits and latents.shape[0] == 2 else shards
    return body(latents, conv_w, embed_w, text_emb, wqkv, seg_ids)


def solution(mesh):
    return jax.shard_map(
        run_shards,
        mesh=mesh,
        in_specs=(
            P("seq", None, None),
            P(None, None, None, "mp"),
            P(None, "mp", "seq"),
            P("seq", "mp"),
            P(None, None, "mp"),
            P(),
        ),
        out_specs=P("seq", "mp"),
        check_vma=False,
    )
```

```python
import functools
import math

import jax
import jax.numpy as jnp
from jax import lax
from jax.experimental import pallas as pl
from jax.experimental.pallas import tpu as pltpu
from jax.sharding import PartitionSpec as P

HD = 128


def padded_2(cells, sides, width):
    for axis, dim in sides:
        count = lax.axis_size(axis)
        ends = count - 1
        head = lax.slice_in_dim(cells, 0, width, axis=dim)
        tail = lax.slice_in_dim(cells, cells.shape[dim] - width, cells.shape[dim], axis=dim)
        cells = jnp.concatenate(
            [
                lax.ppermute(tail, axis, [(i, (i + 1) % count) for i in range(ends)]),
                cells,
                lax.ppermute(head, axis, [((i + 1) % count, i) for i in range(ends)]),
            ],
            axis=dim,
        )
    return cells


def attend_block(carry, pieces, queries, query_pos, query_seg, seg_ids, scale):
    running, totals, outputs = carry
    key_blk, value_blk = pieces
    count = key_blk.shape[0]
    heads = queries.shape[1]
    head_size = queries.shape[2]
    key_heads = key_blk.reshape(count, heads, head_size)
    value_heads = value_blk.reshape(count, heads, head_size)
    key_pos = jnp.arange(count, dtype=jnp.int32)
    allowed = (key_pos[None, :] <= query_pos[:, None]) | (
        query_seg[:, None] == seg_ids[None, :]
    ) & (query_seg[:, None] > 0)
    scores = (
        jnp.einsum("qhd,khd->hqk", queries, key_heads, preferred_element_type=jnp.float32) * scale
    )
    scores = jnp.where(allowed[None], scores, -1e30)
    updated = jnp.maximum(running, jnp.max(scores, axis=-1))
    weights = jnp.where(allowed[None], jnp.exp(scores - updated[..., None]), 0.0)
    totals = jnp.sum(weights, axis=-1)
    probs = weights.astype(jnp.bfloat16)
    outputs = jnp.einsum("hqk,khd->hqd", probs, value_heads, preferred_element_type=jnp.float32)
    return (updated, totals, outputs)


def shards(latents, conv_w, embed_w, text_emb, wqkv, seg_ids):
    tile_rows = latents.shape[0]
    tile_cols = latents.shape[1]
    channels = latents.shape[2]
    chan_dev = conv_w.shape[3]
    patch_rows = tile_rows // 2
    patch_cols = tile_cols // 2
    seq_count = lax.axis_size("seq")
    image_rows = seq_count * patch_rows
    num_images = 1
    tok_rows = text_emb.shape[0]
    total_len = seg_ids.shape[0]
    seq_index = lax.axis_index("seq")
    mp_index = lax.axis_index("mp")
    extended = padded_2(latents, (("seq", 0),), 1)
    first_row = seq_index * tile_rows
    image_height = 2 * image_rows
    keep_top = first_row % image_height != 0
    keep_bottom = (first_row + tile_rows) % image_height != 0
    row_ids = jnp.arange(tile_rows + 2, dtype=jnp.int32)
    keep = jnp.where(row_ids == 0, keep_top, jnp.where(row_ids == tile_rows + 1, keep_bottom, True))
    extended = jnp.where(keep[:, None, None], extended, jnp.zeros_like(extended))
    padded = jnp.pad(extended, ((0, 0), (1, 1), (0, 0)))
    summed = jnp.zeros((tile_rows * tile_cols, chan_dev), jnp.float32)
    for row_step in range(3):
        for col_step in range(3):
            window = padded[
                row_step : row_step + tile_rows, col_step : col_step + tile_cols, :
            ].reshape(tile_rows * tile_cols, channels)
            summed = summed + jnp.dot(
                window, conv_w[row_step, col_step], preferred_element_type=jnp.float32
            )
    own_chan = lax.dynamic_slice_in_dim(latents, mp_index * chan_dev, chan_dev, 2)
    mixed = (
        own_chan.astype(jnp.float32) + jax.nn.silu(summed.reshape(tile_rows, tile_cols, chan_dev))
    ).astype(jnp.bfloat16)
    patches = (
        mixed.reshape(patch_rows, 2, patch_cols, 2, chan_dev)
        .transpose(0, 2, 1, 3, 4)
        .reshape(patch_rows * patch_cols, 4 * chan_dev)
    )
    positions = jnp.arange(total_len, dtype=jnp.int32)
    labels = jnp.arange(1, num_images + 1, dtype=jnp.int32)
    marks = seg_ids[None, :] == labels[:, None]
    starts = jnp.min(jnp.where(marks, positions[None, :], total_len), axis=1)
    base = seq_index * tok_rows
    my_pos = base + jnp.arange(tok_rows, dtype=jnp.int32)
    piece = lax.all_gather(patches, "seq", axis=0, tiled=True)
    count = piece.shape[0]
    token = jnp.arange(count, dtype=jnp.int32)
    row_glob = token // patch_cols
    column = token % patch_cols
    image = row_glob // image_rows
    inner = row_glob % image_rows
    begin = jnp.sum(jnp.where(image[:, None] == labels[None, :] - 1, starts[None, :], 0), axis=1)
    target = begin + inner * patch_cols + column
    select = (my_pos[:, None] == target[None, :]).astype(jnp.bfloat16)
    placed = jnp.dot(select, piece, preferred_element_type=jnp.float32).astype(jnp.bfloat16)
    piece = lax.all_gather(embed_w, "seq", axis=2, tiled=True)
    partial_emb = jnp.dot(
        placed, piece.reshape(4 * chan_dev, piece.shape[2]), preferred_element_type=jnp.float32
    )
    my_seg = lax.dynamic_slice_in_dim(seg_ids, base, tok_rows, 0)
    is_text = my_seg == 0
    feat_dev = text_emb.shape[1]
    text_part = jnp.where(is_text[:, None], text_emb.astype(jnp.float32), 0.0)
    own_cols = lax.dynamic_slice_in_dim(partial_emb, mp_index * feat_dev, feat_dev, 1)
    partial_emb = lax.dynamic_update_slice_in_dim(
        partial_emb, own_cols + text_part, mp_index * feat_dev, 1
    )
    hidden = lax.psum(partial_emb, "mp").astype(jnp.bfloat16)
    width = wqkv.shape[0]
    head_cols = wqkv.shape[2]
    head_size = HD
    heads_dev = head_cols // head_size
    qkv = jnp.dot(
        hidden, wqkv.reshape(width, 3 * head_cols), preferred_element_type=jnp.float32
    ).astype(jnp.bfloat16)
    qkv = qkv.reshape(tok_rows, 3, head_cols)
    queries = qkv[:, 0].reshape(tok_rows, heads_dev, head_size)
    key_rows = qkv[:, 1]
    value_rows = qkv[:, 2]
    scale = head_size ** (-0.5)
    fold_init = (
        jnp.full((heads_dev, tok_rows), -1e30, jnp.float32),
        jnp.zeros((heads_dev, tok_rows), jnp.float32),
        jnp.zeros((heads_dev, tok_rows, head_size), jnp.float32),
    )
    running, totals, outputs = attend_block(
        fold_init,
        (
            lax.all_gather(key_rows, "seq", axis=0, tiled=True),
            lax.all_gather(value_rows, "seq", axis=0, tiled=True),
        ),
        queries,
        my_pos,
        my_seg,
        seg_ids,
        scale,
    )
    result = outputs / totals[..., None]
    return result.transpose(1, 0, 2).reshape(tok_rows, heads_dev * head_size).astype(jnp.bfloat16)


def fused_kernel(
    n_s,
    n_m,
    groups,
    seg_ref,
    lat_ref,
    conv_ref,
    embed_ref,
    text_ref,
    w_ref,
    out_ref,
    w_buf,
    lat_buf,
    conv_buf,
    halo,
    ew,
    text_buf,
    patch_out,
    patch_buf,
    emb_pad,
    emb_out,
    hid_buf,
    acc,
    qkv_out,
    qkv_buf,
    score_buf,
    prob_buf,
    attn_out,
    attn_buf,
    load_sem,
    w_sem,
    halo_send,
    halo_recv,
    ew_send,
    ew_recv,
    text_send,
    text_recv,
    patch_send,
    half_recv,
    patch_recv,
    hid_send,
    hid_recv,
    near_recv,
    qkv_send,
    qkv_recv,
    query_send,
    query_recv,
    attn_send,
    attn_recv,
):
    ranks = n_s // groups
    s = lax.axis_index("seq")
    m = lax.axis_index("mp")
    g = s // ranks
    r = s % ranks
    far = (m + 2) % n_m
    x = m // 2
    c = m % 2
    near = m + 1 - 2 * c
    near_far = (near + 2) % n_m
    cols = lat_ref.shape[1]
    chans = lat_ref.shape[2]
    chan_dev = conv_ref.shape[2]
    half = cols // 2
    tok_rows = text_ref.shape[0]
    width = ew.shape[2]
    img_toks = n_s * half
    total_len = n_s * tok_rows
    pending = []

    def my_cols(core):
        return pl.ds(pl.multiple_of(core * width, width), width)

    def push(src, dst, send, recv, seq, mp):
        copy = pltpu.make_async_remote_copy(
            src_ref=src,
            dst_ref=dst,
            send_sem=send,
            recv_sem=recv,
            device_id=(seq, mp),
            device_id_type=pl.DeviceIdType.MESH,
        )
        copy.start()
        pending.append(copy)

    def arrived(dst, send, recv):
        pltpu.make_async_remote_copy(
            src_ref=dst,
            dst_ref=dst,
            send_sem=send,
            recv_sem=recv,
            device_id=(s, near),
            device_id_type=pl.DeviceIdType.MESH,
        ).wait_recv()

    loads = [
        pltpu.make_async_copy(lat_ref, lat_buf, load_sem.at[0]),
        pltpu.make_async_copy(conv_ref, conv_buf, load_sem.at[1]),
        pltpu.make_async_copy(embed_ref.at[:, my_cols(c)], ew.at[m], load_sem.at[2]),
        pltpu.make_async_copy(text_ref, text_buf.at[m], load_sem.at[3]),
    ]
    for copy in loads:
        copy.start()
    barrier = pltpu.get_barrier_semaphore()
    for step in range(1, n_s):
        pl.semaphore_signal(
            barrier, 1, device_id=((s + step) % n_s, m), device_id_type=pl.DeviceIdType.MESH
        )
    for step in range(1, n_m):
        pl.semaphore_signal(
            barrier, 1, device_id=(s, (m + step) % n_m), device_id_type=pl.DeviceIdType.MESH
        )
    for step in range(1, groups):
        seq = (g + step) % groups * ranks + r
        pl.semaphore_signal(barrier, 1, device_id=(seq, far), device_id_type=pl.DeviceIdType.MESH)
    pl.semaphore_wait(barrier, n_s + n_m + groups - 3)

    loads[0].wait()

    def edge(first, seq):
        return pltpu.make_async_remote_copy(
            src_ref=lat_buf.at[1 - first],
            dst_ref=halo.at[first],
            send_sem=halo_send.at[first],
            recv_sem=halo_recv.at[first],
            device_id=(seq, m),
            device_id_type=pl.DeviceIdType.MESH,
        )

    @pl.when(s < n_s - 1)
    def _():
        edge(0, s + 1).start()

    @pl.when(s > 0)
    def _():
        edge(1, s - 1).start()

    for at, peer in enumerate((far, near_far, near)):
        push(
            embed_ref.at[:, my_cols(peer % 2)],
            ew.at[m],
            ew_send.at[at],
            ew_recv.at[m],
            s,
            peer,
        )

    push(text_ref, text_buf.at[m], text_send.at[1], text_recv.at[m], s, near)

    start_unit = jnp.int32(0)
    before = jnp.int32(1)
    for unit in range((total_len - img_toks) // half):
        before = before * (1 - seg_ref[unit * half])
        start_unit = start_unit + before
    start = start_unit * half

    zero_row = jnp.zeros((cols, chans), jnp.bfloat16)

    @pl.when(s == 0)
    def _():
        halo[0] = zero_row

    @pl.when(s == n_s - 1)
    def _():
        halo[1] = zero_row

    def one_hot(rows, columns, shift):
        row = lax.broadcasted_iota(jnp.int32, (rows, columns), 0)
        column = lax.broadcasted_iota(jnp.int32, (rows, columns), 1)
        return jnp.where(column == shift(row), 1.0, 0.0).astype(jnp.bfloat16)

    picks = one_hot(4 * half, cols, lambda row: 2 * (row % half) + row // half - 1)

    def picked(row):
        return jnp.dot(picks, row, preferred_element_type=jnp.float32).astype(jnp.bfloat16)

    def taps(row, row_step):
        total = None
        for col_step in range(3):
            term = lax.dot_general(
                row[col_step * half : (col_step + 2) * half],
                conv_buf[row_step, col_step],
                (((1,), (1,)), ((), ())),
                preferred_element_type=jnp.float32,
            )
            total = term if total is None else total + term
        return total

    loads[1].wait()
    upper, lower = picked(lat_buf[0]), picked(lat_buf[1])
    sums = [taps(upper, 1) + taps(lower, 2), taps(upper, 0) + taps(lower, 1)]
    row = lax.broadcasted_iota(jnp.int32, (chans, chan_dev), 0)
    column = lax.broadcasted_iota(jnp.int32, (chans, chan_dev), 1)
    own = jnp.where(row == column + m * chan_dev, 1.0, 0.0).astype(jnp.bfloat16)
    own_chan = [
        jnp.dot(line[half : 3 * half], own, preferred_element_type=jnp.float32)
        for line in (upper, lower)
    ]
    places = [
        one_hot(chan_dev, 4 * chan_dev, lambda row, cell=cell: row + cell * chan_dev)
        for cell in range(4)
    ]

    @pl.when(s > 0)
    def _():
        edge(0, s).wait_recv()

    @pl.when(s < n_s - 1)
    def _():
        edge(1, s).wait_recv()

    sums = [sums[0] + taps(picked(halo[0]), 0), sums[1] + taps(picked(halo[1]), 2)]
    patches = jnp.zeros((half, 4 * chan_dev), jnp.float32)
    for line in range(2):
        mixed = (own_chan[line] + sums[line] / (1.0 + jnp.exp(-sums[line]))).astype(jnp.bfloat16)
        for side in range(2):
            patches = patches + jnp.dot(
                mixed[side * half : (side + 1) * half],
                places[2 * line + side],
                preferred_element_type=jnp.float32,
            )

    quarter = half // 2
    first_half = patches[:quarter].astype(jnp.bfloat16)
    second_half = patches[quarter:].astype(jnp.bfloat16)
    patch_buf[s, c, x] = jnp.where(x == 0, first_half, second_half)
    patch_out[...] = jnp.where(x == 0, second_half, first_half)
    sent = [0]

    def send_patch(src, dst, recv, seq, mp):
        push(src, dst, patch_send.at[sent[0]], recv, seq, mp)
        sent[0] += 1

    own_slot = patch_buf.at[s, c, x]
    send_patch(patch_out, own_slot, half_recv.at[s, x], s, far)
    for step in range(1, groups):
        seq = (g + step) % groups * ranks + r
        send_patch(own_slot, own_slot, half_recv.at[s, x], seq, m)
        send_patch(patch_out, own_slot, half_recv.at[s, x], seq, far)
    push(text_ref, text_buf.at[m], text_send.at[0], text_recv.at[m], s, far)
    w_copies = [
        pltpu.make_async_copy(w_ref.at[part], w_buf.at[part], w_sem.at[part]) for part in range(3)
    ]
    for copy in w_copies:
        copy.start()

    def forward_patch(slot, seq, mp):
        pair = patch_buf.at[slot, c]
        send_patch(pair, pair, patch_recv.at[slot, c], seq, mp)

    def wait_patch(slot, core):
        arrived(patch_buf.at[slot, core], patch_send.at[0], patch_recv.at[slot, core])

    for group_step in range(groups):
        slot = (g + groups - group_step) % groups * ranks + r
        if group_step:
            arrived(patch_buf.at[slot, c, x], patch_send.at[0], half_recv.at[slot, x])
        arrived(patch_buf.at[slot, c, 1 - x], patch_send.at[0], half_recv.at[slot, 1 - x])
        for step in range(1, ranks):
            forward_patch(slot, g * ranks + (r + step) % ranks, m)
        forward_patch(slot, s, near)
    for group_step in range(groups):
        for step in range(1, ranks):
            slot = (g + groups - group_step) % groups * ranks + (r + step) % ranks
            wait_patch(slot, c)
            forward_patch(slot, s, near)

    loads[2].wait()
    for peer in (far, near_far, near):
        arrived(ew.at[peer], ew_send.at[0], ew_recv.at[peer])
    for step in range(n_s):
        wait_patch((s + step) % n_s, 1 - c)
    embedded = jnp.zeros((n_s * quarter, width), jnp.float32)
    for group in range(n_m):
        embedded = embedded + jnp.dot(
            patch_buf[:, group % 2, group // 2].reshape(n_s * quarter, 4 * chan_dev),
            ew[group],
            preferred_element_type=jnp.float32,
        )
    pad_units = (total_len - img_toks) // half
    blank = jnp.zeros((pad_units, quarter, width), jnp.bfloat16)
    emb_pad[0:pad_units] = blank
    emb_pad[pad_units : pad_units + n_s] = embedded.astype(jnp.bfloat16).reshape(
        n_s, quarter, width
    )
    emb_pad[pad_units + n_s :] = blank

    per_block = tok_rows // half

    def put_block(ref, seq):
        for unit in range(per_block):
            ref[unit] = emb_pad[pad_units + seq * per_block + unit - start_unit]

    for step in range(1, n_s):
        seq = (s + step) % n_s
        put_block(emb_out.at[seq], seq)
        push(
            emb_out.at[seq],
            hid_buf.at[s, c, x],
            hid_send.at[step - 1],
            hid_recv.at[s, x],
            seq,
            m,
        )
    put_block(hid_buf.at[s, c, x], s)
    for step in range(n_s):
        slot = (s + n_s - step) % n_s
        if step:
            arrived(hid_buf.at[slot, c, x], hid_send.at[0], hid_recv.at[slot, x])
        push(
            hid_buf.at[slot, c, x],
            hid_buf.at[slot, c, x],
            hid_send.at[n_s - 1 + step],
            hid_recv.at[slot, x],
            s,
            far,
        )
    loads[3].wait()
    arrived(text_buf.at[far], text_send.at[0], text_recv.at[far])
    push(text_buf.at[far], text_buf.at[far], text_send.at[2], text_recv.at[far], s, near)
    for step in range(n_s):
        slot = (s + n_s - step) % n_s
        arrived(hid_buf.at[slot, c, 1 - x], hid_send.at[0], hid_recv.at[slot, 1 - x])
        push(
            hid_buf.at[slot, c],
            hid_buf.at[slot, c],
            hid_send.at[2 * n_s - 1 + step],
            near_recv.at[slot],
            s,
            near,
        )
    arrived(text_buf.at[near], text_send.at[0], text_recv.at[near])
    arrived(text_buf.at[near_far], text_send.at[0], text_recv.at[near_far])
    for copy in w_copies:
        copy.wait()
    my_pos = s * tok_rows + lax.broadcasted_iota(jnp.int32, (tok_rows, 1), 0)
    is_image = (my_pos >= start) & (my_pos < start + img_toks)
    per_text = text_ref.shape[1] // width
    deep = 2 * width
    for step in range(n_s):
        slot = (s + n_s - step) % n_s
        arrived(hid_buf.at[slot, 1 - c], hid_send.at[0], near_recv.at[slot])
        pieces = []
        for core in range(2):
            chunk = slot * 2 + core
            text = text_buf[
                chunk // per_text,
                :,
                pl.ds(pl.multiple_of(chunk % per_text * width, width), width),
            ]
            image = jnp.concatenate(
                [hid_buf[slot, core, side, unit] for unit in range(per_block) for side in range(2)],
                axis=0,
            )
            pieces.append(jnp.where(is_image, image, text))
        hidden = jnp.concatenate(pieces, axis=1)
        for part in range(3):
            product = jnp.dot(
                hidden,
                w_buf[part, pl.ds(pl.multiple_of(slot * deep, deep), deep)],
                preferred_element_type=jnp.float32,
            )
            if step == 0:
                acc[part] = product
            else:
                acc[part] += product

    for head in range(groups):
        for part in range(3):
            qkv_out[head, :, part * HD : (part + 1) * HD] = acc[
                part, :, head * HD : (head + 1) * HD
            ].astype(jnp.bfloat16)
    sent_qkv = [0]

    def send_qkv(src, dst, slot, seq):
        push(src, dst, qkv_send.at[sent_qkv[0]], qkv_recv.at[slot], seq, m)
        sent_qkv[0] += 1

    key_cols = pl.ds(HD, 2 * HD)
    query_cols = pl.ds(0, HD)
    for step in range(1, groups):
        head = (g + step) % groups
        send_qkv(
            qkv_out.at[head, :, key_cols], qkv_buf.at[s, :, key_cols], s, head * ranks + r
        )
    qkv_buf[s] = qkv_out[g]
    for step in range(1, ranks):
        kv = qkv_buf.at[s, :, key_cols]
        send_qkv(kv, kv, s, g * ranks + (r + step) % ranks)
    for step in range(1, groups):
        head = (g + step) % groups
        push(
            qkv_out.at[head, :, query_cols],
            qkv_buf.at[s, :, query_cols],
            query_send.at[step - 1],
            query_recv.at[s],
            head * ranks + r,
            m,
        )
    for group_step in range(1, groups):
        slot = (g + groups - group_step) % groups * ranks + r
        kv = qkv_buf.at[slot, :, key_cols]
        arrived(kv, qkv_send.at[0], qkv_recv.at[slot])
        for step in range(1, ranks):
            send_qkv(kv, kv, slot, g * ranks + (r + step) % ranks)

    done = len(pending) - groups * ranks - groups
    for copy in pending[:done]:
        copy.wait_send()
    del pending[:done]

    @pl.when(s < n_s - 1)
    def _():
        edge(0, s).wait_send()

    @pl.when(s > 0)
    def _():
        edge(1, s).wait_send()

    for group_step in range(1, groups):
        slot = (g + groups - group_step) % groups * ranks + r
        arrived(qkv_buf.at[slot, :, query_cols], query_send.at[0], query_recv.at[slot])
    for group_step in range(groups):
        for step in range(1, ranks):
            slot = (g + groups - group_step) % groups * ranks + (r + step) % ranks
            arrived(qkv_buf.at[slot, :, key_cols], qkv_send.at[0], qkv_recv.at[slot])

    keys = qkv_buf[:, :, HD : 2 * HD].reshape(total_len, HD)
    values = qkv_buf[:, :, 2 * HD :].reshape(total_len, HD)
    order = [*range(1, groups), 0]
    queries = jnp.concatenate(
        [qkv_buf[(g + step) % groups * ranks + r, :, :HD] for step in order], axis=0
    )
    score_buf[...] = lax.dot_general(
        queries, keys, (((1,), (1,)), ((), ())), preferred_element_type=jnp.float32
    )
    tile = min(32, tok_rows)
    key_pos = lax.broadcasted_iota(jnp.int32, (tile, total_len), 1)
    for at, group_step in enumerate(order):
        other = (g + group_step) % groups
        slot = other * ranks + r
        totals = []
        for row in range(0, tok_rows, tile):
            query_pos = slot * tok_rows + row + lax.broadcasted_iota(jnp.int32, (tile, 1), 0)
            query_image = (query_pos >= start) & (query_pos < start + img_toks)
            last_seen = jnp.where(query_image, start + img_toks - 1, query_pos)
            scores = score_buf[at * tok_rows + row : at * tok_rows + row + tile]
            scores = jnp.where(key_pos <= last_seen, scores, -1e30)
            highest = jnp.max(scores, axis=1, keepdims=True)
            weights = jnp.exp2((scores - highest) * (HD**-0.5 * math.log2(math.e)))
            totals.append(jnp.sum(weights, axis=1, keepdims=True))
            prob_buf[row : row + tile] = weights.astype(jnp.bfloat16)
        result = jnp.dot(prob_buf[...], values, preferred_element_type=jnp.float32)
        result = (result / jnp.concatenate(totals, axis=0)).astype(jnp.bfloat16)
        if group_step:
            attn_out[other] = result
            push(
                attn_out.at[other],
                attn_buf.at[g],
                attn_send.at[group_step - 1],
                attn_recv.at[g],
                slot,
                m,
            )
        else:
            attn_buf[g] = result
    for group_step in range(1, groups):
        other = (g + group_step) % groups
        arrived(attn_buf.at[other], attn_send.at[0], attn_recv.at[other])
    for head in range(groups):
        out_ref[:, head * HD : (head + 1) * HD] = attn_buf[head]
    for copy in pending:
        copy.wait_send()


def fused_shards(latents, conv_w, embed_w, text_emb, wqkv, seg_ids):
    n_s = lax.axis_size("seq")
    n_m = lax.axis_size("mp")
    tile_rows, cols, chans = latents.shape
    chan_dev = conv_w.shape[3]
    tok_rows, feats = text_emb.shape
    groups = wqkv.shape[2] // HD
    ranks = n_s // groups
    width = embed_w.shape[2] // 2
    half = cols // 2
    total_len = seg_ids.shape[0]
    img_toks = n_s * half
    bf16 = jnp.bfloat16
    vmem = pl.BlockSpec(memory_space=pltpu.VMEM)
    hbm = pl.BlockSpec(memory_space=pltpu.HBM)
    dma = pltpu.SemaphoreType.DMA
    return pl.pallas_call(
        functools.partial(fused_kernel, n_s, n_m, groups),
        out_shape=pltpu.VMEM((tok_rows, groups * HD), bf16),
        in_specs=[
            pl.BlockSpec(memory_space=pltpu.SMEM),
            hbm,
            hbm,
            hbm,
            hbm,
            hbm,
        ],
        out_specs=vmem,
        scratch_shapes=[
            pltpu.VMEM((3, wqkv.shape[0], wqkv.shape[2]), bf16),
            pltpu.VMEM((2, cols, chans), bf16),
            pltpu.VMEM((3, 3, chan_dev, chans), bf16),
            pltpu.VMEM((2, cols, chans), bf16),
            pltpu.VMEM((n_m, 4 * chan_dev, width), bf16),
            pltpu.VMEM((n_m, tok_rows, feats), bf16),
            pltpu.VMEM((half // 2, 4 * chan_dev), bf16),
            pltpu.VMEM((n_s, 2, 2, half // 2, 4 * chan_dev), bf16),
            pltpu.VMEM(((2 * total_len - img_toks) // half, half // 2, width), bf16),
            pltpu.VMEM((n_s, tok_rows // half, half // 2, width), bf16),
            pltpu.VMEM((n_s, 2, 2, tok_rows // half, half // 2, width), bf16),
            pltpu.VMEM((3, tok_rows, wqkv.shape[2]), jnp.float32),
            pltpu.VMEM((groups, tok_rows, 3 * HD), bf16),
            pltpu.VMEM((n_s, tok_rows, 3 * HD), bf16),
            pltpu.VMEM((groups * tok_rows, total_len), jnp.float32),
            pltpu.VMEM((tok_rows, total_len), bf16),
            pltpu.VMEM((groups, tok_rows, HD), bf16),
            pltpu.VMEM((groups, tok_rows, HD), bf16),
            dma((4,)),
            dma((3,)),
            dma((2,)),
            dma((2,)),
            dma((n_m - 1,)),
            dma((n_m,)),
            dma((3,)),
            dma((n_m,)),
            dma((1 + 2 * (groups - 1) + groups * (ranks - 1) + n_s,)),
            dma((n_s, 2)),
            dma((n_s, 2)),
            dma((n_s - 1 + 2 * n_s,)),
            dma((n_s, 2)),
            dma((n_s,)),
            dma((groups - 1 + groups * (ranks - 1),)),
            dma((n_s,)),
            dma((groups - 1,)),
            dma((n_s,)),
            dma((groups - 1,)),
            dma((groups,)),
        ],
        compiler_params=pltpu.CompilerParams(
            collective_id=0, has_side_effects=True, vmem_limit_bytes=60 * 1024 * 1024
        ),
        cost_estimate=pl.CostEstimate(
            flops=2 * tok_rows * wqkv.shape[0] * 3 * wqkv.shape[2],
            bytes_accessed=2 * wqkv.shape[0] * 3 * wqkv.shape[2],
            transcendentals=tok_rows * total_len * groups,
        ),
    )(
        seg_ids,
        latents,
        conv_w.transpose(0, 1, 3, 2),
        embed_w.reshape(4 * chan_dev, embed_w.shape[2]),
        text_emb,
        wqkv.transpose(1, 0, 2),
    )


def run_shards(latents, conv_w, embed_w, text_emb, wqkv, seg_ids):
    n_s = lax.axis_size("seq")
    n_m = lax.axis_size("mp")
    groups = wqkv.shape[2] // HD
    fits = n_m == 4 and n_s % groups == 0 and embed_w.shape[2] % (2 * HD) == 0
    body = fused_shards if fits and latents.shape[0] == 2 else shards
    return body(latents, conv_w, embed_w, text_emb, wqkv, seg_ids)


def solution(mesh):
    return jax.shard_map(
        run_shards,
        mesh=mesh,
        in_specs=(
            P("seq", None, None),
            P(None, None, None, "mp"),
            P(None, "mp", "seq"),
            P("seq", "mp"),
            P(None, None, "mp"),
            P(),
        ),
        out_specs=P("seq", "mp"),
        check_vma=False,
    )
```

```python
import functools
import math

import jax
import jax.numpy as jnp
from jax import lax
from jax.experimental import pallas as pl
from jax.experimental.pallas import tpu as pltpu
from jax.sharding import PartitionSpec as P

HD = 128


def padded_2(cells, sides, width):
    for axis, dim in sides:
        count = lax.axis_size(axis)
        ends = count - 1
        head = lax.slice_in_dim(cells, 0, width, axis=dim)
        tail = lax.slice_in_dim(cells, cells.shape[dim] - width, cells.shape[dim], axis=dim)
        cells = jnp.concatenate(
            [
                lax.ppermute(tail, axis, [(i, (i + 1) % count) for i in range(ends)]),
                cells,
                lax.ppermute(head, axis, [((i + 1) % count, i) for i in range(ends)]),
            ],
            axis=dim,
        )
    return cells


def attend_block(carry, pieces, queries, query_pos, query_seg, seg_ids, scale):
    running, totals, outputs = carry
    key_blk, value_blk = pieces
    count = key_blk.shape[0]
    heads = queries.shape[1]
    head_size = queries.shape[2]
    key_heads = key_blk.reshape(count, heads, head_size)
    value_heads = value_blk.reshape(count, heads, head_size)
    key_pos = jnp.arange(count, dtype=jnp.int32)
    allowed = (key_pos[None, :] <= query_pos[:, None]) | (
        query_seg[:, None] == seg_ids[None, :]
    ) & (query_seg[:, None] > 0)
    scores = (
        jnp.einsum("qhd,khd->hqk", queries, key_heads, preferred_element_type=jnp.float32) * scale
    )
    scores = jnp.where(allowed[None], scores, -1e30)
    updated = jnp.maximum(running, jnp.max(scores, axis=-1))
    weights = jnp.where(allowed[None], jnp.exp(scores - updated[..., None]), 0.0)
    totals = jnp.sum(weights, axis=-1)
    probs = weights.astype(jnp.bfloat16)
    outputs = jnp.einsum("hqk,khd->hqd", probs, value_heads, preferred_element_type=jnp.float32)
    return (updated, totals, outputs)


def shards(latents, conv_w, embed_w, text_emb, wqkv, seg_ids):
    tile_rows = latents.shape[0]
    tile_cols = latents.shape[1]
    channels = latents.shape[2]
    chan_dev = conv_w.shape[3]
    patch_rows = tile_rows // 2
    patch_cols = tile_cols // 2
    seq_count = lax.axis_size("seq")
    image_rows = seq_count * patch_rows
    num_images = 1
    tok_rows = text_emb.shape[0]
    total_len = seg_ids.shape[0]
    seq_index = lax.axis_index("seq")
    mp_index = lax.axis_index("mp")
    extended = padded_2(latents, (("seq", 0),), 1)
    first_row = seq_index * tile_rows
    image_height = 2 * image_rows
    keep_top = first_row % image_height != 0
    keep_bottom = (first_row + tile_rows) % image_height != 0
    row_ids = jnp.arange(tile_rows + 2, dtype=jnp.int32)
    keep = jnp.where(row_ids == 0, keep_top, jnp.where(row_ids == tile_rows + 1, keep_bottom, True))
    extended = jnp.where(keep[:, None, None], extended, jnp.zeros_like(extended))
    padded = jnp.pad(extended, ((0, 0), (1, 1), (0, 0)))
    summed = jnp.zeros((tile_rows * tile_cols, chan_dev), jnp.float32)
    for row_step in range(3):
        for col_step in range(3):
            window = padded[
                row_step : row_step + tile_rows, col_step : col_step + tile_cols, :
            ].reshape(tile_rows * tile_cols, channels)
            summed = summed + jnp.dot(
                window, conv_w[row_step, col_step], preferred_element_type=jnp.float32
            )
    own_chan = lax.dynamic_slice_in_dim(latents, mp_index * chan_dev, chan_dev, 2)
    mixed = (
        own_chan.astype(jnp.float32) + jax.nn.silu(summed.reshape(tile_rows, tile_cols, chan_dev))
    ).astype(jnp.bfloat16)
    patches = (
        mixed.reshape(patch_rows, 2, patch_cols, 2, chan_dev)
        .transpose(0, 2, 1, 3, 4)
        .reshape(patch_rows * patch_cols, 4 * chan_dev)
    )
    positions = jnp.arange(total_len, dtype=jnp.int32)
    labels = jnp.arange(1, num_images + 1, dtype=jnp.int32)
    marks = seg_ids[None, :] == labels[:, None]
    starts = jnp.min(jnp.where(marks, positions[None, :], total_len), axis=1)
    base = seq_index * tok_rows
    my_pos = base + jnp.arange(tok_rows, dtype=jnp.int32)
    piece = lax.all_gather(patches, "seq", axis=0, tiled=True)
    count = piece.shape[0]
    token = jnp.arange(count, dtype=jnp.int32)
    row_glob = token // patch_cols
    column = token % patch_cols
    image = row_glob // image_rows
    inner = row_glob % image_rows
    begin = jnp.sum(jnp.where(image[:, None] == labels[None, :] - 1, starts[None, :], 0), axis=1)
    target = begin + inner * patch_cols + column
    select = (my_pos[:, None] == target[None, :]).astype(jnp.bfloat16)
    placed = jnp.dot(select, piece, preferred_element_type=jnp.float32).astype(jnp.bfloat16)
    piece = lax.all_gather(embed_w, "seq", axis=2, tiled=True)
    partial_emb = jnp.dot(
        placed, piece.reshape(4 * chan_dev, piece.shape[2]), preferred_element_type=jnp.float32
    )
    my_seg = lax.dynamic_slice_in_dim(seg_ids, base, tok_rows, 0)
    is_text = my_seg == 0
    feat_dev = text_emb.shape[1]
    text_part = jnp.where(is_text[:, None], text_emb.astype(jnp.float32), 0.0)
    own_cols = lax.dynamic_slice_in_dim(partial_emb, mp_index * feat_dev, feat_dev, 1)
    partial_emb = lax.dynamic_update_slice_in_dim(
        partial_emb, own_cols + text_part, mp_index * feat_dev, 1
    )
    hidden = lax.psum(partial_emb, "mp").astype(jnp.bfloat16)
    width = wqkv.shape[0]
    head_cols = wqkv.shape[2]
    head_size = HD
    heads_dev = head_cols // head_size
    qkv = jnp.dot(
        hidden, wqkv.reshape(width, 3 * head_cols), preferred_element_type=jnp.float32
    ).astype(jnp.bfloat16)
    qkv = qkv.reshape(tok_rows, 3, head_cols)
    queries = qkv[:, 0].reshape(tok_rows, heads_dev, head_size)
    key_rows = qkv[:, 1]
    value_rows = qkv[:, 2]
    scale = head_size ** (-0.5)
    fold_init = (
        jnp.full((heads_dev, tok_rows), -1e30, jnp.float32),
        jnp.zeros((heads_dev, tok_rows), jnp.float32),
        jnp.zeros((heads_dev, tok_rows, head_size), jnp.float32),
    )
    running, totals, outputs = attend_block(
        fold_init,
        (
            lax.all_gather(key_rows, "seq", axis=0, tiled=True),
            lax.all_gather(value_rows, "seq", axis=0, tiled=True),
        ),
        queries,
        my_pos,
        my_seg,
        seg_ids,
        scale,
    )
    result = outputs / totals[..., None]
    return result.transpose(1, 0, 2).reshape(tok_rows, heads_dev * head_size).astype(jnp.bfloat16)


def fused_kernel(
    n_s,
    n_m,
    groups,
    seg_ref,
    lat_ref,
    conv_ref,
    embed_ref,
    text_ref,
    w_ref,
    out_ref,
    w_buf,
    lat_buf,
    conv_buf,
    halo,
    ew,
    text_buf,
    patch_out,
    patch_buf,
    emb_pad,
    emb_out,
    hid_buf,
    hid_rows,
    acc,
    qkv_out,
    qkv_buf,
    score_buf,
    prob_buf,
    attn_out,
    attn_buf,
    load_sem,
    w_sem,
    halo_send,
    halo_recv,
    ew_send,
    ew_recv,
    text_send,
    text_recv,
    patch_send,
    half_recv,
    patch_recv,
    hid_send,
    hid_recv,
    near_recv,
    qkv_send,
    qkv_recv,
    query_send,
    query_recv,
    attn_send,
    attn_recv,
):
    ranks = n_s // groups
    s = lax.axis_index("seq")
    m = lax.axis_index("mp")
    g = s // ranks
    r = s % ranks
    far = (m + 2) % n_m
    x = m // 2
    c = m % 2
    near = m + 1 - 2 * c
    near_far = (near + 2) % n_m
    cols = lat_ref.shape[1]
    chans = lat_ref.shape[2]
    chan_dev = conv_ref.shape[2]
    half = cols // 2
    tok_rows = text_ref.shape[0]
    width = ew.shape[2]
    img_toks = n_s * half
    total_len = n_s * tok_rows
    pending = []

    def my_cols(core):
        return pl.ds(pl.multiple_of(core * width, width), width)

    def push(src, dst, send, recv, seq, mp):
        copy = pltpu.make_async_remote_copy(
            src_ref=src,
            dst_ref=dst,
            send_sem=send,
            recv_sem=recv,
            device_id=(seq, mp),
            device_id_type=pl.DeviceIdType.MESH,
        )
        copy.start()
        pending.append(copy)

    def arrived(dst, send, recv):
        pltpu.make_async_remote_copy(
            src_ref=dst,
            dst_ref=dst,
            send_sem=send,
            recv_sem=recv,
            device_id=(s, near),
            device_id_type=pl.DeviceIdType.MESH,
        ).wait_recv()

    loads = [
        pltpu.make_async_copy(lat_ref, lat_buf, load_sem.at[0]),
        pltpu.make_async_copy(conv_ref, conv_buf, load_sem.at[1]),
        pltpu.make_async_copy(embed_ref.at[:, my_cols(c)], ew.at[m], load_sem.at[2]),
        pltpu.make_async_copy(text_ref, text_buf.at[m], load_sem.at[3]),
    ]
    for copy in loads:
        copy.start()
    barrier = pltpu.get_barrier_semaphore()
    for step in range(1, n_s):
        pl.semaphore_signal(
            barrier, 1, device_id=((s + step) % n_s, m), device_id_type=pl.DeviceIdType.MESH
        )
    for step in range(1, n_m):
        pl.semaphore_signal(
            barrier, 1, device_id=(s, (m + step) % n_m), device_id_type=pl.DeviceIdType.MESH
        )
    for step in range(1, groups):
        seq = (g + step) % groups * ranks + r
        pl.semaphore_signal(barrier, 1, device_id=(seq, far), device_id_type=pl.DeviceIdType.MESH)
    pl.semaphore_wait(barrier, n_s + n_m + groups - 3)

    loads[0].wait()

    def edge(first, seq):
        return pltpu.make_async_remote_copy(
            src_ref=lat_buf.at[1 - first],
            dst_ref=halo.at[first],
            send_sem=halo_send.at[first],
            recv_sem=halo_recv.at[first],
            device_id=(seq, m),
            device_id_type=pl.DeviceIdType.MESH,
        )

    @pl.when(s < n_s - 1)
    def _():
        edge(0, s + 1).start()

    @pl.when(s > 0)
    def _():
        edge(1, s - 1).start()

    for at, peer in enumerate((far, near_far, near)):
        push(
            embed_ref.at[:, my_cols(peer % 2)],
            ew.at[m],
            ew_send.at[at],
            ew_recv.at[m],
            s,
            peer,
        )

    push(text_ref, text_buf.at[m], text_send.at[1], text_recv.at[m], s, near)

    start_unit = jnp.int32(0)
    before = jnp.int32(1)
    for unit in range((total_len - img_toks) // half):
        before = before * (1 - seg_ref[unit * half])
        start_unit = start_unit + before
    start = start_unit * half

    zero_row = jnp.zeros((cols, chans), jnp.bfloat16)

    @pl.when(s == 0)
    def _():
        halo[0] = zero_row

    @pl.when(s == n_s - 1)
    def _():
        halo[1] = zero_row

    def one_hot(rows, columns, shift):
        row = lax.broadcasted_iota(jnp.int32, (rows, columns), 0)
        column = lax.broadcasted_iota(jnp.int32, (rows, columns), 1)
        return jnp.where(column == shift(row), 1.0, 0.0).astype(jnp.bfloat16)

    picks = one_hot(4 * half, cols, lambda row: 2 * (row % half) + row // half - 1)

    def picked(row):
        return jnp.dot(picks, row, preferred_element_type=jnp.float32).astype(jnp.bfloat16)

    def taps(row, row_step):
        total = None
        for col_step in range(3):
            term = lax.dot_general(
                row[col_step * half : (col_step + 2) * half],
                conv_buf[row_step, col_step],
                (((1,), (1,)), ((), ())),
                preferred_element_type=jnp.float32,
            )
            total = term if total is None else total + term
        return total

    loads[1].wait()
    upper, lower = picked(lat_buf[0]), picked(lat_buf[1])
    sums = [taps(upper, 1) + taps(lower, 2), taps(upper, 0) + taps(lower, 1)]
    row = lax.broadcasted_iota(jnp.int32, (chans, chan_dev), 0)
    column = lax.broadcasted_iota(jnp.int32, (chans, chan_dev), 1)
    own = jnp.where(row == column + m * chan_dev, 1.0, 0.0).astype(jnp.bfloat16)
    own_chan = [
        jnp.dot(line[half : 3 * half], own, preferred_element_type=jnp.float32)
        for line in (upper, lower)
    ]
    places = [
        one_hot(chan_dev, 4 * chan_dev, lambda row, cell=cell: row + cell * chan_dev)
        for cell in range(4)
    ]

    @pl.when(s > 0)
    def _():
        edge(0, s).wait_recv()

    @pl.when(s < n_s - 1)
    def _():
        edge(1, s).wait_recv()

    sums = [sums[0] + taps(picked(halo[0]), 0), sums[1] + taps(picked(halo[1]), 2)]
    patches = jnp.zeros((half, 4 * chan_dev), jnp.float32)
    for line in range(2):
        mixed = (own_chan[line] + sums[line] / (1.0 + jnp.exp(-sums[line]))).astype(jnp.bfloat16)
        for side in range(2):
            patches = patches + jnp.dot(
                mixed[side * half : (side + 1) * half],
                places[2 * line + side],
                preferred_element_type=jnp.float32,
            )

    quarter = half // 2
    first_half = patches[:quarter].astype(jnp.bfloat16)
    second_half = patches[quarter:].astype(jnp.bfloat16)
    patch_buf[s, c, x] = jnp.where(x == 0, first_half, second_half)
    patch_out[...] = jnp.where(x == 0, second_half, first_half)
    sent = [0]

    def send_patch(src, dst, recv, seq, mp):
        push(src, dst, patch_send.at[sent[0]], recv, seq, mp)
        sent[0] += 1

    own_slot = patch_buf.at[s, c, x]
    send_patch(patch_out, own_slot, half_recv.at[s, x], s, far)
    for step in range(1, groups):
        seq = (g + step) % groups * ranks + r
        send_patch(own_slot, own_slot, half_recv.at[s, x], seq, m)
        send_patch(patch_out, own_slot, half_recv.at[s, x], seq, far)
    push(text_ref, text_buf.at[m], text_send.at[0], text_recv.at[m], s, far)
    w_copies = [
        pltpu.make_async_copy(w_ref.at[part], w_buf.at[part], w_sem.at[part]) for part in range(3)
    ]
    for copy in w_copies:
        copy.start()

    def forward_patch(slot, seq, mp):
        pair = patch_buf.at[slot, c]
        send_patch(pair, pair, patch_recv.at[slot, c], seq, mp)

    def wait_patch(slot, core):
        arrived(patch_buf.at[slot, core], patch_send.at[0], patch_recv.at[slot, core])

    for group_step in range(groups):
        slot = (g + groups - group_step) % groups * ranks + r
        if group_step:
            arrived(patch_buf.at[slot, c, x], patch_send.at[0], half_recv.at[slot, x])
        arrived(patch_buf.at[slot, c, 1 - x], patch_send.at[0], half_recv.at[slot, 1 - x])
        for step in range(1, ranks):
            forward_patch(slot, g * ranks + (r + step) % ranks, m)
        forward_patch(slot, s, near)
    for group_step in range(groups):
        for step in range(1, ranks):
            slot = (g + groups - group_step) % groups * ranks + (r + step) % ranks
            wait_patch(slot, c)
            forward_patch(slot, s, near)

    loads[2].wait()
    for peer in (far, near_far, near):
        arrived(ew.at[peer], ew_send.at[0], ew_recv.at[peer])
    for step in range(n_s):
        wait_patch((s + step) % n_s, 1 - c)
    embedded = jnp.zeros((n_s * quarter, width), jnp.float32)
    for group in range(n_m):
        embedded = embedded + jnp.dot(
            patch_buf[:, group % 2, group // 2].reshape(n_s * quarter, 4 * chan_dev),
            ew[group],
            preferred_element_type=jnp.float32,
        )
    pad_units = (total_len - img_toks) // half
    blank = jnp.zeros((pad_units, quarter, width), jnp.bfloat16)
    emb_pad[0:pad_units] = blank
    emb_pad[pad_units : pad_units + n_s] = embedded.astype(jnp.bfloat16).reshape(
        n_s, quarter, width
    )
    emb_pad[pad_units + n_s :] = blank

    per_block = tok_rows // half

    def put_block(ref, seq):
        for unit in range(per_block):
            ref[unit] = emb_pad[pad_units + seq * per_block + unit - start_unit]

    for step in range(1, n_s):
        seq = (s + step) % n_s
        put_block(emb_out.at[seq], seq)
        push(
            emb_out.at[seq],
            hid_buf.at[s, c, x],
            hid_send.at[step - 1],
            hid_recv.at[s, x],
            seq,
            m,
        )
    put_block(hid_buf.at[s, c, x], s)
    loads[3].wait()
    arrived(text_buf.at[far], text_send.at[0], text_recv.at[far])
    push(text_buf.at[far], text_buf.at[far], text_send.at[2], text_recv.at[far], s, near)
    for step in range(n_s):
        slot = (s + n_s - step) % n_s
        if step:
            arrived(hid_buf.at[slot, c, x], hid_send.at[0], hid_recv.at[slot, x])
        push(
            hid_buf.at[slot, c, x],
            hid_buf.at[slot, c, x],
            hid_send.at[n_s - 1 + step],
            hid_recv.at[slot, x],
            s,
            far,
        )
    for step in range(n_s):
        slot = (s + n_s - step) % n_s
        arrived(hid_buf.at[slot, c, 1 - x], hid_send.at[0], hid_recv.at[slot, 1 - x])
        push(
            hid_buf.at[slot, c],
            hid_buf.at[slot, c],
            hid_send.at[2 * n_s - 1 + step],
            near_recv.at[slot],
            s,
            near,
        )
    arrived(text_buf.at[near], text_send.at[0], text_recv.at[near])
    arrived(text_buf.at[near_far], text_send.at[0], text_recv.at[near_far])
    for copy in w_copies:
        copy.wait()
    my_pos = s * tok_rows + lax.broadcasted_iota(jnp.int32, (tok_rows, 1), 0)
    is_image = (my_pos >= start) & (my_pos < start + img_toks)
    per_text = text_ref.shape[1] // width
    deep = 2 * width

    def project(part, slot, hidden, first):
        product = jnp.dot(
            hidden,
            w_buf[part, pl.ds(pl.multiple_of(slot * deep, deep), deep)],
            preferred_element_type=jnp.float32,
        )
        if first:
            acc[part] = product
        else:
            acc[part] += product

    for step in range(n_s):
        slot = (s + n_s - step) % n_s
        arrived(hid_buf.at[slot, 1 - c], hid_send.at[0], near_recv.at[slot])
        pieces = []
        for core in range(2):
            chunk = slot * 2 + core
            text = text_buf[
                chunk // per_text,
                :,
                pl.ds(pl.multiple_of(chunk % per_text * width, width), width),
            ]
            image = jnp.concatenate(
                [hid_buf[slot, core, side, unit] for unit in range(per_block) for side in range(2)],
                axis=0,
            )
            pieces.append(jnp.where(is_image, image, text))
        hidden = jnp.concatenate(pieces, axis=1)
        hid_rows[slot] = hidden
        for part in range(1, 3):
            project(part, slot, hidden, step == 0)

    def cast_head(head, part):
        at = pl.ds(pl.multiple_of(head * HD, HD), HD)
        qkv_out[head, :, part * HD : (part + 1) * HD] = acc[part, :, at].astype(jnp.bfloat16)

    sent_qkv = [0]

    def send_qkv(src, dst, slot, seq):
        push(src, dst, qkv_send.at[sent_qkv[0]], qkv_recv.at[slot], seq, m)
        sent_qkv[0] += 1

    key_cols = pl.ds(HD, 2 * HD)
    query_cols = pl.ds(0, HD)
    for step in range(1, groups):
        head = (g + step) % groups
        cast_head(head, 1)
        cast_head(head, 2)
        send_qkv(
            qkv_out.at[head, :, key_cols], qkv_buf.at[s, :, key_cols], s, head * ranks + r
        )
    cast_head(g, 1)
    cast_head(g, 2)
    qkv_buf[s, :, key_cols] = qkv_out[g, :, key_cols]
    for step in range(1, ranks):
        kv = qkv_buf.at[s, :, key_cols]
        send_qkv(kv, kv, s, g * ranks + (r + step) % ranks)
    for slot in range(n_s):
        project(0, slot, hid_rows[slot], slot == 0)
    cast_head(g, 0)
    qkv_buf[s, :, query_cols] = qkv_out[g, :, query_cols]
    for step in range(1, groups):
        head = (g + step) % groups
        cast_head(head, 0)
        push(
            qkv_out.at[head, :, query_cols],
            qkv_buf.at[s, :, query_cols],
            query_send.at[step - 1],
            query_recv.at[s],
            head * ranks + r,
            m,
        )
    for group_step in range(1, groups):
        slot = (g + groups - group_step) % groups * ranks + r
        kv = qkv_buf.at[slot, :, key_cols]
        arrived(kv, qkv_send.at[0], qkv_recv.at[slot])
        for step in range(1, ranks):
            send_qkv(kv, kv, slot, g * ranks + (r + step) % ranks)

    done = len(pending) - groups * ranks - groups
    for copy in pending[:done]:
        copy.wait_send()
    del pending[:done]

    @pl.when(s < n_s - 1)
    def _():
        edge(0, s).wait_send()

    @pl.when(s > 0)
    def _():
        edge(1, s).wait_send()

    for group_step in range(1, groups):
        slot = (g + groups - group_step) % groups * ranks + r
        arrived(qkv_buf.at[slot, :, query_cols], query_send.at[0], query_recv.at[slot])
    for group_step in range(groups):
        for step in range(1, ranks):
            slot = (g + groups - group_step) % groups * ranks + (r + step) % ranks
            arrived(qkv_buf.at[slot, :, key_cols], qkv_send.at[0], qkv_recv.at[slot])

    keys = qkv_buf[:, :, HD : 2 * HD].reshape(total_len, HD)
    values = qkv_buf[:, :, 2 * HD :].reshape(total_len, HD)
    order = [*range(1, groups), 0]
    queries = jnp.concatenate(
        [qkv_buf[(g + step) % groups * ranks + r, :, :HD] for step in order], axis=0
    )
    score_buf[...] = lax.dot_general(
        queries, keys, (((1,), (1,)), ((), ())), preferred_element_type=jnp.float32
    )
    tile = min(32, tok_rows)
    key_pos = lax.broadcasted_iota(jnp.int32, (tile, total_len), 1)
    for at, group_step in enumerate(order):
        other = (g + group_step) % groups
        slot = other * ranks + r
        totals = []
        for row in range(0, tok_rows, tile):
            query_pos = slot * tok_rows + row + lax.broadcasted_iota(jnp.int32, (tile, 1), 0)
            query_image = (query_pos >= start) & (query_pos < start + img_toks)
            last_seen = jnp.where(query_image, start + img_toks - 1, query_pos)
            scores = score_buf[at * tok_rows + row : at * tok_rows + row + tile]
            scores = jnp.where(key_pos <= last_seen, scores, -1e30)
            highest = jnp.max(scores, axis=1, keepdims=True)
            weights = jnp.exp2((scores - highest) * (HD**-0.5 * math.log2(math.e)))
            totals.append(jnp.sum(weights, axis=1, keepdims=True))
            prob_buf[row : row + tile] = weights.astype(jnp.bfloat16)
        result = jnp.dot(prob_buf[...], values, preferred_element_type=jnp.float32)
        result = (result / jnp.concatenate(totals, axis=0)).astype(jnp.bfloat16)
        if group_step:
            attn_out[other] = result
            push(
                attn_out.at[other],
                attn_buf.at[g],
                attn_send.at[group_step - 1],
                attn_recv.at[g],
                slot,
                m,
            )
        else:
            attn_buf[g] = result
    for group_step in range(1, groups):
        other = (g + group_step) % groups
        arrived(attn_buf.at[other], attn_send.at[0], attn_recv.at[other])
    for head in range(groups):
        out_ref[:, head * HD : (head + 1) * HD] = attn_buf[head]
    for copy in pending:
        copy.wait_send()


def fused_shards(latents, conv_w, embed_w, text_emb, wqkv, seg_ids):
    n_s = lax.axis_size("seq")
    n_m = lax.axis_size("mp")
    tile_rows, cols, chans = latents.shape
    chan_dev = conv_w.shape[3]
    tok_rows, feats = text_emb.shape
    groups = wqkv.shape[2] // HD
    ranks = n_s // groups
    width = embed_w.shape[2] // 2
    half = cols // 2
    total_len = seg_ids.shape[0]
    img_toks = n_s * half
    bf16 = jnp.bfloat16
    vmem = pl.BlockSpec(memory_space=pltpu.VMEM)
    hbm = pl.BlockSpec(memory_space=pltpu.HBM)
    dma = pltpu.SemaphoreType.DMA
    return pl.pallas_call(
        functools.partial(fused_kernel, n_s, n_m, groups),
        out_shape=pltpu.VMEM((tok_rows, groups * HD), bf16),
        in_specs=[
            pl.BlockSpec(memory_space=pltpu.SMEM),
            hbm,
            hbm,
            hbm,
            hbm,
            hbm,
        ],
        out_specs=vmem,
        scratch_shapes=[
            pltpu.VMEM((3, wqkv.shape[0], wqkv.shape[2]), bf16),
            pltpu.VMEM((2, cols, chans), bf16),
            pltpu.VMEM((3, 3, chan_dev, chans), bf16),
            pltpu.VMEM((2, cols, chans), bf16),
            pltpu.VMEM((n_m, 4 * chan_dev, width), bf16),
            pltpu.VMEM((n_m, tok_rows, feats), bf16),
            pltpu.VMEM((half // 2, 4 * chan_dev), bf16),
            pltpu.VMEM((n_s, 2, 2, half // 2, 4 * chan_dev), bf16),
            pltpu.VMEM(((2 * total_len - img_toks) // half, half // 2, width), bf16),
            pltpu.VMEM((n_s, tok_rows // half, half // 2, width), bf16),
            pltpu.VMEM((n_s, 2, 2, tok_rows // half, half // 2, width), bf16),
            pltpu.VMEM((n_s, tok_rows, 2 * width), bf16),
            pltpu.VMEM((3, tok_rows, wqkv.shape[2]), jnp.float32),
            pltpu.VMEM((groups, tok_rows, 3 * HD), bf16),
            pltpu.VMEM((n_s, tok_rows, 3 * HD), bf16),
            pltpu.VMEM((groups * tok_rows, total_len), jnp.float32),
            pltpu.VMEM((tok_rows, total_len), bf16),
            pltpu.VMEM((groups, tok_rows, HD), bf16),
            pltpu.VMEM((groups, tok_rows, HD), bf16),
            dma((4,)),
            dma((3,)),
            dma((2,)),
            dma((2,)),
            dma((n_m - 1,)),
            dma((n_m,)),
            dma((3,)),
            dma((n_m,)),
            dma((1 + 2 * (groups - 1) + groups * (ranks - 1) + n_s,)),
            dma((n_s, 2)),
            dma((n_s, 2)),
            dma((n_s - 1 + 2 * n_s,)),
            dma((n_s, 2)),
            dma((n_s,)),
            dma((groups - 1 + groups * (ranks - 1),)),
            dma((n_s,)),
            dma((groups - 1,)),
            dma((n_s,)),
            dma((groups - 1,)),
            dma((groups,)),
        ],
        compiler_params=pltpu.CompilerParams(
            collective_id=0, has_side_effects=True, vmem_limit_bytes=60 * 1024 * 1024
        ),
        cost_estimate=pl.CostEstimate(
            flops=2 * tok_rows * wqkv.shape[0] * 3 * wqkv.shape[2],
            bytes_accessed=2 * wqkv.shape[0] * 3 * wqkv.shape[2],
            transcendentals=tok_rows * total_len * groups,
        ),
    )(
        seg_ids,
        latents,
        conv_w.transpose(0, 1, 3, 2),
        embed_w.reshape(4 * chan_dev, embed_w.shape[2]),
        text_emb,
        wqkv.transpose(1, 0, 2),
    )


def run_shards(latents, conv_w, embed_w, text_emb, wqkv, seg_ids):
    n_s = lax.axis_size("seq")
    n_m = lax.axis_size("mp")
    groups = wqkv.shape[2] // HD
    fits = n_m == 4 and n_s % groups == 0 and embed_w.shape[2] % (2 * HD) == 0
    body = fused_shards if fits and latents.shape[0] == 2 else shards
    return body(latents, conv_w, embed_w, text_emb, wqkv, seg_ids)


def solution(mesh):
    return jax.shard_map(
        run_shards,
        mesh=mesh,
        in_specs=(
            P("seq", None, None),
            P(None, None, None, "mp"),
            P(None, "mp", "seq"),
            P("seq", "mp"),
            P(None, None, "mp"),
            P(),
        ),
        out_specs=P("seq", "mp"),
        check_vma=False,
    )
```

```python
import functools
import math

import jax
import jax.numpy as jnp
from jax import lax
from jax.experimental import pallas as pl
from jax.experimental.pallas import tpu as pltpu
from jax.sharding import PartitionSpec as P

HD = 128


def padded_2(cells, sides, width):
    for axis, dim in sides:
        count = lax.axis_size(axis)
        ends = count - 1
        head = lax.slice_in_dim(cells, 0, width, axis=dim)
        tail = lax.slice_in_dim(cells, cells.shape[dim] - width, cells.shape[dim], axis=dim)
        cells = jnp.concatenate(
            [
                lax.ppermute(tail, axis, [(i, (i + 1) % count) for i in range(ends)]),
                cells,
                lax.ppermute(head, axis, [((i + 1) % count, i) for i in range(ends)]),
            ],
            axis=dim,
        )
    return cells


def attend_block(carry, pieces, queries, query_pos, query_seg, seg_ids, scale):
    running, totals, outputs = carry
    key_blk, value_blk = pieces
    count = key_blk.shape[0]
    heads = queries.shape[1]
    head_size = queries.shape[2]
    key_heads = key_blk.reshape(count, heads, head_size)
    value_heads = value_blk.reshape(count, heads, head_size)
    key_pos = jnp.arange(count, dtype=jnp.int32)
    allowed = (key_pos[None, :] <= query_pos[:, None]) | (
        query_seg[:, None] == seg_ids[None, :]
    ) & (query_seg[:, None] > 0)
    scores = (
        jnp.einsum("qhd,khd->hqk", queries, key_heads, preferred_element_type=jnp.float32) * scale
    )
    scores = jnp.where(allowed[None], scores, -1e30)
    updated = jnp.maximum(running, jnp.max(scores, axis=-1))
    weights = jnp.where(allowed[None], jnp.exp(scores - updated[..., None]), 0.0)
    totals = jnp.sum(weights, axis=-1)
    probs = weights.astype(jnp.bfloat16)
    outputs = jnp.einsum("hqk,khd->hqd", probs, value_heads, preferred_element_type=jnp.float32)
    return (updated, totals, outputs)


def shards(latents, conv_w, embed_w, text_emb, wqkv, seg_ids):
    tile_rows = latents.shape[0]
    tile_cols = latents.shape[1]
    channels = latents.shape[2]
    chan_dev = conv_w.shape[3]
    patch_rows = tile_rows // 2
    patch_cols = tile_cols // 2
    seq_count = lax.axis_size("seq")
    image_rows = seq_count * patch_rows
    num_images = 1
    tok_rows = text_emb.shape[0]
    total_len = seg_ids.shape[0]
    seq_index = lax.axis_index("seq")
    mp_index = lax.axis_index("mp")
    extended = padded_2(latents, (("seq", 0),), 1)
    first_row = seq_index * tile_rows
    image_height = 2 * image_rows
    keep_top = first_row % image_height != 0
    keep_bottom = (first_row + tile_rows) % image_height != 0
    row_ids = jnp.arange(tile_rows + 2, dtype=jnp.int32)
    keep = jnp.where(row_ids == 0, keep_top, jnp.where(row_ids == tile_rows + 1, keep_bottom, True))
    extended = jnp.where(keep[:, None, None], extended, jnp.zeros_like(extended))
    padded = jnp.pad(extended, ((0, 0), (1, 1), (0, 0)))
    summed = jnp.zeros((tile_rows * tile_cols, chan_dev), jnp.float32)
    for row_step in range(3):
        for col_step in range(3):
            window = padded[
                row_step : row_step + tile_rows, col_step : col_step + tile_cols, :
            ].reshape(tile_rows * tile_cols, channels)
            summed = summed + jnp.dot(
                window, conv_w[row_step, col_step], preferred_element_type=jnp.float32
            )
    own_chan = lax.dynamic_slice_in_dim(latents, mp_index * chan_dev, chan_dev, 2)
    mixed = (
        own_chan.astype(jnp.float32) + jax.nn.silu(summed.reshape(tile_rows, tile_cols, chan_dev))
    ).astype(jnp.bfloat16)
    patches = (
        mixed.reshape(patch_rows, 2, patch_cols, 2, chan_dev)
        .transpose(0, 2, 1, 3, 4)
        .reshape(patch_rows * patch_cols, 4 * chan_dev)
    )
    positions = jnp.arange(total_len, dtype=jnp.int32)
    labels = jnp.arange(1, num_images + 1, dtype=jnp.int32)
    marks = seg_ids[None, :] == labels[:, None]
    starts = jnp.min(jnp.where(marks, positions[None, :], total_len), axis=1)
    base = seq_index * tok_rows
    my_pos = base + jnp.arange(tok_rows, dtype=jnp.int32)
    piece = lax.all_gather(patches, "seq", axis=0, tiled=True)
    count = piece.shape[0]
    token = jnp.arange(count, dtype=jnp.int32)
    row_glob = token // patch_cols
    column = token % patch_cols
    image = row_glob // image_rows
    inner = row_glob % image_rows
    begin = jnp.sum(jnp.where(image[:, None] == labels[None, :] - 1, starts[None, :], 0), axis=1)
    target = begin + inner * patch_cols + column
    select = (my_pos[:, None] == target[None, :]).astype(jnp.bfloat16)
    placed = jnp.dot(select, piece, preferred_element_type=jnp.float32).astype(jnp.bfloat16)
    piece = lax.all_gather(embed_w, "seq", axis=2, tiled=True)
    partial_emb = jnp.dot(
        placed, piece.reshape(4 * chan_dev, piece.shape[2]), preferred_element_type=jnp.float32
    )
    my_seg = lax.dynamic_slice_in_dim(seg_ids, base, tok_rows, 0)
    is_text = my_seg == 0
    feat_dev = text_emb.shape[1]
    text_part = jnp.where(is_text[:, None], text_emb.astype(jnp.float32), 0.0)
    own_cols = lax.dynamic_slice_in_dim(partial_emb, mp_index * feat_dev, feat_dev, 1)
    partial_emb = lax.dynamic_update_slice_in_dim(
        partial_emb, own_cols + text_part, mp_index * feat_dev, 1
    )
    hidden = lax.psum(partial_emb, "mp").astype(jnp.bfloat16)
    width = wqkv.shape[0]
    head_cols = wqkv.shape[2]
    head_size = HD
    heads_dev = head_cols // head_size
    qkv = jnp.dot(
        hidden, wqkv.reshape(width, 3 * head_cols), preferred_element_type=jnp.float32
    ).astype(jnp.bfloat16)
    qkv = qkv.reshape(tok_rows, 3, head_cols)
    queries = qkv[:, 0].reshape(tok_rows, heads_dev, head_size)
    key_rows = qkv[:, 1]
    value_rows = qkv[:, 2]
    scale = head_size ** (-0.5)
    fold_init = (
        jnp.full((heads_dev, tok_rows), -1e30, jnp.float32),
        jnp.zeros((heads_dev, tok_rows), jnp.float32),
        jnp.zeros((heads_dev, tok_rows, head_size), jnp.float32),
    )
    running, totals, outputs = attend_block(
        fold_init,
        (
            lax.all_gather(key_rows, "seq", axis=0, tiled=True),
            lax.all_gather(value_rows, "seq", axis=0, tiled=True),
        ),
        queries,
        my_pos,
        my_seg,
        seg_ids,
        scale,
    )
    result = outputs / totals[..., None]
    return result.transpose(1, 0, 2).reshape(tok_rows, heads_dev * head_size).astype(jnp.bfloat16)


def fused_kernel(
    n_s,
    n_m,
    groups,
    seg_ref,
    lat_ref,
    conv_ref,
    embed_ref,
    text_ref,
    w_ref,
    out_ref,
    w_buf,
    lat_buf,
    conv_buf,
    halo,
    ew,
    text_buf,
    patch_out,
    patch_buf,
    emb_pad,
    emb_out,
    hid_buf,
    hid_rows,
    acc,
    qkv_out,
    qkv_buf,
    score_buf,
    prob_buf,
    attn_out,
    attn_buf,
    load_sem,
    w_sem,
    halo_send,
    halo_recv,
    ew_send,
    ew_recv,
    text_send,
    text_recv,
    patch_send,
    half_recv,
    patch_recv,
    hid_send,
    hid_recv,
    near_recv,
    qkv_send,
    qkv_recv,
    query_send,
    query_recv,
    attn_send,
    attn_recv,
):
    ranks = n_s // groups
    s = lax.axis_index("seq")
    m = lax.axis_index("mp")
    g = s // ranks
    r = s % ranks
    far = (m + 2) % n_m
    x = m // 2
    c = m % 2
    near = m + 1 - 2 * c
    near_far = (near + 2) % n_m
    cols = lat_ref.shape[1]
    chans = lat_ref.shape[2]
    chan_dev = conv_ref.shape[2]
    half = cols // 2
    tok_rows = text_ref.shape[0]
    width = ew.shape[2]
    img_toks = n_s * half
    total_len = n_s * tok_rows
    pending = []

    def my_cols(core):
        return pl.ds(pl.multiple_of(core * width, width), width)

    def push(src, dst, send, recv, seq, mp):
        copy = pltpu.make_async_remote_copy(
            src_ref=src,
            dst_ref=dst,
            send_sem=send,
            recv_sem=recv,
            device_id=(seq, mp),
            device_id_type=pl.DeviceIdType.MESH,
        )
        copy.start()
        pending.append(copy)

    def arrived(dst, send, recv):
        pltpu.make_async_remote_copy(
            src_ref=dst,
            dst_ref=dst,
            send_sem=send,
            recv_sem=recv,
            device_id=(s, near),
            device_id_type=pl.DeviceIdType.MESH,
        ).wait_recv()

    loads = [
        pltpu.make_async_copy(lat_ref, lat_buf, load_sem.at[0]),
        pltpu.make_async_copy(conv_ref, conv_buf, load_sem.at[1]),
        pltpu.make_async_copy(embed_ref.at[:, my_cols(c)], ew.at[m], load_sem.at[2]),
        pltpu.make_async_copy(text_ref, text_buf.at[m], load_sem.at[3]),
    ]
    for copy in loads:
        copy.start()
    barrier = pltpu.get_barrier_semaphore()
    for step in range(1, n_s):
        pl.semaphore_signal(
            barrier, 1, device_id=((s + step) % n_s, m), device_id_type=pl.DeviceIdType.MESH
        )
    for step in range(1, n_m):
        pl.semaphore_signal(
            barrier, 1, device_id=(s, (m + step) % n_m), device_id_type=pl.DeviceIdType.MESH
        )
    for step in range(1, groups):
        seq = (g + step) % groups * ranks + r
        pl.semaphore_signal(barrier, 1, device_id=(seq, far), device_id_type=pl.DeviceIdType.MESH)
    pl.semaphore_wait(barrier, n_s + n_m + groups - 3)

    loads[0].wait()

    def edge(first, seq):
        return pltpu.make_async_remote_copy(
            src_ref=lat_buf.at[1 - first],
            dst_ref=halo.at[first],
            send_sem=halo_send.at[first],
            recv_sem=halo_recv.at[first],
            device_id=(seq, m),
            device_id_type=pl.DeviceIdType.MESH,
        )

    @pl.when(s < n_s - 1)
    def _():
        edge(0, s + 1).start()

    @pl.when(s > 0)
    def _():
        edge(1, s - 1).start()

    for at, peer in enumerate((far, near_far, near)):
        push(
            embed_ref.at[:, my_cols(peer % 2)],
            ew.at[m],
            ew_send.at[at],
            ew_recv.at[m],
            s,
            peer,
        )

    push(text_ref, text_buf.at[m], text_send.at[1], text_recv.at[m], s, near)

    start_unit = jnp.int32(0)
    before = jnp.int32(1)
    for unit in range((total_len - img_toks) // half):
        before = before * (1 - seg_ref[unit * half])
        start_unit = start_unit + before
    start = start_unit * half

    zero_row = jnp.zeros((cols, chans), jnp.bfloat16)

    @pl.when(s == 0)
    def _():
        halo[0] = zero_row

    @pl.when(s == n_s - 1)
    def _():
        halo[1] = zero_row

    def one_hot(rows, columns, shift):
        row = lax.broadcasted_iota(jnp.int32, (rows, columns), 0)
        column = lax.broadcasted_iota(jnp.int32, (rows, columns), 1)
        return jnp.where(column == shift(row), 1.0, 0.0).astype(jnp.bfloat16)

    picks = one_hot(4 * half, cols, lambda row: 2 * (row % half) + row // half - 1)

    def picked(row):
        return jnp.dot(picks, row, preferred_element_type=jnp.float32).astype(jnp.bfloat16)

    def taps(row, row_step):
        total = None
        for col_step in range(3):
            term = lax.dot_general(
                row[col_step * half : (col_step + 2) * half],
                conv_buf[row_step, col_step],
                (((1,), (1,)), ((), ())),
                preferred_element_type=jnp.float32,
            )
            total = term if total is None else total + term
        return total

    loads[1].wait()
    upper, lower = picked(lat_buf[0]), picked(lat_buf[1])
    sums = [taps(upper, 1) + taps(lower, 2), taps(upper, 0) + taps(lower, 1)]
    row = lax.broadcasted_iota(jnp.int32, (chans, chan_dev), 0)
    column = lax.broadcasted_iota(jnp.int32, (chans, chan_dev), 1)
    own = jnp.where(row == column + m * chan_dev, 1.0, 0.0).astype(jnp.bfloat16)
    own_chan = [
        jnp.dot(line[half : 3 * half], own, preferred_element_type=jnp.float32)
        for line in (upper, lower)
    ]
    places = [
        one_hot(chan_dev, 4 * chan_dev, lambda row, cell=cell: row + cell * chan_dev)
        for cell in range(4)
    ]

    @pl.when(s > 0)
    def _():
        edge(0, s).wait_recv()

    @pl.when(s < n_s - 1)
    def _():
        edge(1, s).wait_recv()

    sums = [sums[0] + taps(picked(halo[0]), 0), sums[1] + taps(picked(halo[1]), 2)]
    patches = jnp.zeros((half, 4 * chan_dev), jnp.float32)
    for line in range(2):
        mixed = (own_chan[line] + sums[line] / (1.0 + jnp.exp(-sums[line]))).astype(jnp.bfloat16)
        for side in range(2):
            patches = patches + jnp.dot(
                mixed[side * half : (side + 1) * half],
                places[2 * line + side],
                preferred_element_type=jnp.float32,
            )

    quarter = half // 2
    first_half = patches[:quarter].astype(jnp.bfloat16)
    second_half = patches[quarter:].astype(jnp.bfloat16)
    patch_buf[s, c, x] = jnp.where(x == 0, first_half, second_half)
    patch_out[...] = jnp.where(x == 0, second_half, first_half)
    sent = [0]

    def send_patch(src, dst, recv, seq, mp):
        push(src, dst, patch_send.at[sent[0]], recv, seq, mp)
        sent[0] += 1

    own_slot = patch_buf.at[s, c, x]
    send_patch(patch_out, own_slot, half_recv.at[s, x], s, far)
    for step in range(1, groups):
        seq = (g + step) % groups * ranks + r
        send_patch(own_slot, own_slot, half_recv.at[s, x], seq, m)
        send_patch(patch_out, own_slot, half_recv.at[s, x], seq, far)
    push(text_ref, text_buf.at[m], text_send.at[0], text_recv.at[m], s, far)
    w_copies = [
        pltpu.make_async_copy(w_ref.at[part], w_buf.at[part], w_sem.at[part]) for part in range(3)
    ]
    for copy in w_copies:
        copy.start()

    def forward_patch(slot, seq, mp):
        pair = patch_buf.at[slot, c]
        send_patch(pair, pair, patch_recv.at[slot, c], seq, mp)

    def wait_patch(slot, core):
        arrived(patch_buf.at[slot, core], patch_send.at[0], patch_recv.at[slot, core])

    for group_step in range(groups):
        slot = (g + groups - group_step) % groups * ranks + r
        if group_step:
            arrived(patch_buf.at[slot, c, x], patch_send.at[0], half_recv.at[slot, x])
        arrived(patch_buf.at[slot, c, 1 - x], patch_send.at[0], half_recv.at[slot, 1 - x])
        for step in range(1, ranks):
            forward_patch(slot, g * ranks + (r + step) % ranks, m)
        forward_patch(slot, s, near)
    for group_step in range(groups):
        for step in range(1, ranks):
            slot = (g + groups - group_step) % groups * ranks + (r + step) % ranks
            wait_patch(slot, c)
            forward_patch(slot, s, near)

    loads[2].wait()
    for peer in (far, near_far, near):
        arrived(ew.at[peer], ew_send.at[0], ew_recv.at[peer])
    for step in range(n_s):
        wait_patch((s + step) % n_s, 1 - c)
    embedded = jnp.zeros((n_s * quarter, width), jnp.float32)
    for group in range(n_m):
        embedded = embedded + jnp.dot(
            patch_buf[:, group % 2, group // 2].reshape(n_s * quarter, 4 * chan_dev),
            ew[group],
            preferred_element_type=jnp.float32,
        )
    pad_units = (total_len - img_toks) // half
    blank = jnp.zeros((pad_units, quarter, width), jnp.bfloat16)
    emb_pad[0:pad_units] = blank
    emb_pad[pad_units : pad_units + n_s] = embedded.astype(jnp.bfloat16).reshape(
        n_s, quarter, width
    )
    emb_pad[pad_units + n_s :] = blank

    per_block = tok_rows // half

    def put_block(ref, seq):
        for unit in range(per_block):
            ref[unit] = emb_pad[pad_units + seq * per_block + unit - start_unit]

    for step in range(1, n_s):
        seq = (s + step) % n_s
        put_block(emb_out.at[seq], seq)
        push(
            emb_out.at[seq],
            hid_buf.at[s, c, x],
            hid_send.at[step - 1],
            hid_recv.at[s, x],
            seq,
            m,
        )
    put_block(hid_buf.at[s, c, x], s)
    loads[3].wait()
    arrived(text_buf.at[far], text_send.at[0], text_recv.at[far])
    push(text_buf.at[far], text_buf.at[far], text_send.at[2], text_recv.at[far], s, near)
    for step in range(n_s):
        slot = (s + n_s - step) % n_s
        if step:
            arrived(hid_buf.at[slot, c, x], hid_send.at[0], hid_recv.at[slot, x])
        push(
            hid_buf.at[slot, c, x],
            hid_buf.at[slot, c, x],
            hid_send.at[n_s - 1 + step],
            hid_recv.at[slot, x],
            s,
            far,
        )
    def to_near(step):
        slot = (s + n_s - step) % n_s
        arrived(hid_buf.at[slot, c, 1 - x], hid_send.at[0], hid_recv.at[slot, 1 - x])
        push(
            hid_buf.at[slot, c],
            hid_buf.at[slot, c],
            hid_send.at[2 * n_s - 1 + step],
            near_recv.at[slot],
            s,
            near,
        )

    late = 2
    for step in range(n_s - late):
        to_near(step)
    arrived(text_buf.at[near], text_send.at[0], text_recv.at[near])
    arrived(text_buf.at[near_far], text_send.at[0], text_recv.at[near_far])
    for copy in w_copies:
        copy.wait()
    my_pos = s * tok_rows + lax.broadcasted_iota(jnp.int32, (tok_rows, 1), 0)
    is_image = (my_pos >= start) & (my_pos < start + img_toks)
    per_text = text_ref.shape[1] // width
    deep = 2 * width

    def project(part, slot, hidden, first):
        product = jnp.dot(
            hidden,
            w_buf[part, pl.ds(pl.multiple_of(slot * deep, deep), deep)],
            preferred_element_type=jnp.float32,
        )
        if first:
            acc[part] = product
        else:
            acc[part] += product

    for step in range(n_s):
        slot = (s + n_s - step) % n_s
        arrived(hid_buf.at[slot, 1 - c], hid_send.at[0], near_recv.at[slot])
        pieces = []
        for core in range(2):
            chunk = slot * 2 + core
            text = text_buf[
                chunk // per_text,
                :,
                pl.ds(pl.multiple_of(chunk % per_text * width, width), width),
            ]
            image = jnp.concatenate(
                [hid_buf[slot, core, side, unit] for unit in range(per_block) for side in range(2)],
                axis=0,
            )
            pieces.append(jnp.where(is_image, image, text))
        hidden = jnp.concatenate(pieces, axis=1)
        hid_rows[slot] = hidden
        for part in range(1, 3):
            project(part, slot, hidden, step == 0)
        if step < late:
            to_near(n_s - late + step)

    def cast_head(head, part):
        at = pl.ds(pl.multiple_of(head * HD, HD), HD)
        qkv_out[head, :, part * HD : (part + 1) * HD] = acc[part, :, at].astype(jnp.bfloat16)

    sent_qkv = [0]

    def send_qkv(src, dst, slot, seq):
        push(src, dst, qkv_send.at[sent_qkv[0]], qkv_recv.at[slot], seq, m)
        sent_qkv[0] += 1

    key_cols = pl.ds(HD, 2 * HD)
    query_cols = pl.ds(0, HD)
    for step in range(1, groups):
        head = (g + step) % groups
        cast_head(head, 1)
        cast_head(head, 2)
        send_qkv(
            qkv_out.at[head, :, key_cols], qkv_buf.at[s, :, key_cols], s, head * ranks + r
        )
    cast_head(g, 1)
    cast_head(g, 2)
    qkv_buf[s, :, key_cols] = qkv_out[g, :, key_cols]
    for step in range(1, ranks):
        kv = qkv_buf.at[s, :, key_cols]
        send_qkv(kv, kv, s, g * ranks + (r + step) % ranks)
    for slot in range(n_s):
        project(0, slot, hid_rows[slot], slot == 0)
    cast_head(g, 0)
    qkv_buf[s, :, query_cols] = qkv_out[g, :, query_cols]
    for step in range(1, groups):
        head = (g + step) % groups
        cast_head(head, 0)
        push(
            qkv_out.at[head, :, query_cols],
            qkv_buf.at[s, :, query_cols],
            query_send.at[step - 1],
            query_recv.at[s],
            head * ranks + r,
            m,
        )
    for group_step in range(1, groups):
        slot = (g + groups - group_step) % groups * ranks + r
        kv = qkv_buf.at[slot, :, key_cols]
        arrived(kv, qkv_send.at[0], qkv_recv.at[slot])
        for step in range(1, ranks):
            send_qkv(kv, kv, slot, g * ranks + (r + step) % ranks)

    done = len(pending) - groups * ranks - groups
    for copy in pending[:done]:
        copy.wait_send()
    del pending[:done]

    @pl.when(s < n_s - 1)
    def _():
        edge(0, s).wait_send()

    @pl.when(s > 0)
    def _():
        edge(1, s).wait_send()

    for group_step in range(1, groups):
        slot = (g + groups - group_step) % groups * ranks + r
        arrived(qkv_buf.at[slot, :, query_cols], query_send.at[0], query_recv.at[slot])
    for group_step in range(groups):
        for step in range(1, ranks):
            slot = (g + groups - group_step) % groups * ranks + (r + step) % ranks
            arrived(qkv_buf.at[slot, :, key_cols], qkv_send.at[0], qkv_recv.at[slot])

    keys = qkv_buf[:, :, HD : 2 * HD].reshape(total_len, HD)
    values = qkv_buf[:, :, 2 * HD :].reshape(total_len, HD)
    order = [*range(1, groups), 0]
    queries = jnp.concatenate(
        [qkv_buf[(g + step) % groups * ranks + r, :, :HD] for step in order], axis=0
    )
    score_buf[...] = lax.dot_general(
        queries, keys, (((1,), (1,)), ((), ())), preferred_element_type=jnp.float32
    )
    tile = min(32, tok_rows)
    key_pos = lax.broadcasted_iota(jnp.int32, (tile, total_len), 1)
    for at, group_step in enumerate(order):
        other = (g + group_step) % groups
        slot = other * ranks + r
        totals = []
        for row in range(0, tok_rows, tile):
            query_pos = slot * tok_rows + row + lax.broadcasted_iota(jnp.int32, (tile, 1), 0)
            query_image = (query_pos >= start) & (query_pos < start + img_toks)
            last_seen = jnp.where(query_image, start + img_toks - 1, query_pos)
            scores = score_buf[at * tok_rows + row : at * tok_rows + row + tile]
            scores = jnp.where(key_pos <= last_seen, scores, -1e30)
            highest = jnp.max(scores, axis=1, keepdims=True)
            weights = jnp.exp2((scores - highest) * (HD**-0.5 * math.log2(math.e)))
            totals.append(jnp.sum(weights, axis=1, keepdims=True))
            prob_buf[row : row + tile] = weights.astype(jnp.bfloat16)
        result = jnp.dot(prob_buf[...], values, preferred_element_type=jnp.float32)
        result = (result / jnp.concatenate(totals, axis=0)).astype(jnp.bfloat16)
        if group_step:
            attn_out[other] = result
            push(
                attn_out.at[other],
                attn_buf.at[g],
                attn_send.at[group_step - 1],
                attn_recv.at[g],
                slot,
                m,
            )
        else:
            attn_buf[g] = result
    for group_step in range(1, groups):
        other = (g + group_step) % groups
        arrived(attn_buf.at[other], attn_send.at[0], attn_recv.at[other])
    for head in range(groups):
        out_ref[:, head * HD : (head + 1) * HD] = attn_buf[head]
    for copy in pending:
        copy.wait_send()


def fused_shards(latents, conv_w, embed_w, text_emb, wqkv, seg_ids):
    n_s = lax.axis_size("seq")
    n_m = lax.axis_size("mp")
    tile_rows, cols, chans = latents.shape
    chan_dev = conv_w.shape[3]
    tok_rows, feats = text_emb.shape
    groups = wqkv.shape[2] // HD
    ranks = n_s // groups
    width = embed_w.shape[2] // 2
    half = cols // 2
    total_len = seg_ids.shape[0]
    img_toks = n_s * half
    bf16 = jnp.bfloat16
    vmem = pl.BlockSpec(memory_space=pltpu.VMEM)
    hbm = pl.BlockSpec(memory_space=pltpu.HBM)
    dma = pltpu.SemaphoreType.DMA
    return pl.pallas_call(
        functools.partial(fused_kernel, n_s, n_m, groups),
        out_shape=pltpu.VMEM((tok_rows, groups * HD), bf16),
        in_specs=[
            pl.BlockSpec(memory_space=pltpu.SMEM),
            hbm,
            hbm,
            hbm,
            hbm,
            hbm,
        ],
        out_specs=vmem,
        scratch_shapes=[
            pltpu.VMEM((3, wqkv.shape[0], wqkv.shape[2]), bf16),
            pltpu.VMEM((2, cols, chans), bf16),
            pltpu.VMEM((3, 3, chan_dev, chans), bf16),
            pltpu.VMEM((2, cols, chans), bf16),
            pltpu.VMEM((n_m, 4 * chan_dev, width), bf16),
            pltpu.VMEM((n_m, tok_rows, feats), bf16),
            pltpu.VMEM((half // 2, 4 * chan_dev), bf16),
            pltpu.VMEM((n_s, 2, 2, half // 2, 4 * chan_dev), bf16),
            pltpu.VMEM(((2 * total_len - img_toks) // half, half // 2, width), bf16),
            pltpu.VMEM((n_s, tok_rows // half, half // 2, width), bf16),
            pltpu.VMEM((n_s, 2, 2, tok_rows // half, half // 2, width), bf16),
            pltpu.VMEM((n_s, tok_rows, 2 * width), bf16),
            pltpu.VMEM((3, tok_rows, wqkv.shape[2]), jnp.float32),
            pltpu.VMEM((groups, tok_rows, 3 * HD), bf16),
            pltpu.VMEM((n_s, tok_rows, 3 * HD), bf16),
            pltpu.VMEM((groups * tok_rows, total_len), jnp.float32),
            pltpu.VMEM((tok_rows, total_len), bf16),
            pltpu.VMEM((groups, tok_rows, HD), bf16),
            pltpu.VMEM((groups, tok_rows, HD), bf16),
            dma((4,)),
            dma((3,)),
            dma((2,)),
            dma((2,)),
            dma((n_m - 1,)),
            dma((n_m,)),
            dma((3,)),
            dma((n_m,)),
            dma((1 + 2 * (groups - 1) + groups * (ranks - 1) + n_s,)),
            dma((n_s, 2)),
            dma((n_s, 2)),
            dma((n_s - 1 + 2 * n_s,)),
            dma((n_s, 2)),
            dma((n_s,)),
            dma((groups - 1 + groups * (ranks - 1),)),
            dma((n_s,)),
            dma((groups - 1,)),
            dma((n_s,)),
            dma((groups - 1,)),
            dma((groups,)),
        ],
        compiler_params=pltpu.CompilerParams(
            collective_id=0, has_side_effects=True, vmem_limit_bytes=60 * 1024 * 1024
        ),
        cost_estimate=pl.CostEstimate(
            flops=2 * tok_rows * wqkv.shape[0] * 3 * wqkv.shape[2],
            bytes_accessed=2 * wqkv.shape[0] * 3 * wqkv.shape[2],
            transcendentals=tok_rows * total_len * groups,
        ),
    )(
        seg_ids,
        latents,
        conv_w.transpose(0, 1, 3, 2),
        embed_w.reshape(4 * chan_dev, embed_w.shape[2]),
        text_emb,
        wqkv.transpose(1, 0, 2),
    )


def run_shards(latents, conv_w, embed_w, text_emb, wqkv, seg_ids):
    n_s = lax.axis_size("seq")
    n_m = lax.axis_size("mp")
    groups = wqkv.shape[2] // HD
    fits = n_m == 4 and n_s % groups == 0 and embed_w.shape[2] % (2 * HD) == 0
    body = fused_shards if fits and latents.shape[0] == 2 else shards
    return body(latents, conv_w, embed_w, text_emb, wqkv, seg_ids)


def solution(mesh):
    return jax.shard_map(
        run_shards,
        mesh=mesh,
        in_specs=(
            P("seq", None, None),
            P(None, None, None, "mp"),
            P(None, "mp", "seq"),
            P("seq", "mp"),
            P(None, None, "mp"),
            P(),
        ),
        out_specs=P("seq", "mp"),
        check_vma=False,
    )
```
